256 devices in a mesh: dp: 8 (over z_lo, y), ctx: 32 (over x, z_hi, core).
Axes of the slice: x: 4, y: 4, z: 8 (z_hi: 4, z_lo: 2; z = z_hi * 2 + z_lo), core: 2. Of those that a mesh axis runs over, the one named last changes fastest.
Arguments:
- queries: bfloat16 [8, 8192, 2048], P('dp', 'ctx'), may hold values from -40 to 40
- keys: bfloat16 [8, 8192, 2048], P('dp', 'ctx'), may hold values from -40 to 40
- values: bfloat16 [8, 8192, 2048], P('dp', 'ctx'), may hold values from -6 to 6
- out_grad: bfloat16 [8, 8192, 4096], P('dp', 'ctx'), may hold values from -6 to 6
- q_init: bfloat16 [64, 4096], replicated, may hold values from -0.09375 to 0.09375
- lengths: int32 [8], P('dp'), may hold values from 4096 to 8192, as said below
Outputs:
- p_hat: float32 [64, 2048], replicated
- q_new: float32 [64, 4096], replicated
The draws below stay inside these ranges and needn't reach their ends.
Inputs may be any that keep to these rules, and one draw needn't show every extreme that they name: `lengths`: one stream in every draw is valid over all its frames.
All inputs are finite; a program needn't handle non-finite values.
Results may differ from the reference program's by a relative error of at most 0.008.
Values may be sent and summed in bfloat16 or wider, within the bound.
A program may use at most 128 MiB of HBM per device.

```python
import jax
import jax.numpy as jnp
from jax import lax

HEADS = 16
HEAD_DIM = 128
D = 4096
RANK = 64
WINDOW = 2048
FR_DEV = 256
HD = 2048
SEQ = 8192
N_DP = 8


def shared_base(key):
    return jax.random.normal(key, (N_DP, SEQ, HD), jnp.float32)


def draw_keys(key, part):
    base = shared_base(key)
    result = base
    return jnp.clip(result, -40.0, 40.0).astype(jnp.bfloat16)


def draw_queries(key, part):
    key = jax.random.fold_in(key, 23)
    result = jax.random.normal(key, (N_DP, SEQ, HD), jnp.float32)
    return jnp.clip(result, -40.0, 40.0).astype(jnp.bfloat16)


def draw_lengths(key, part):
    key = jax.random.fold_in(key, 5)
    first, second = jax.random.split(key)
    drawn = jax.random.randint(first, (N_DP,), SEQ // 2, SEQ + 1, dtype=jnp.int32)
    full = jax.random.randint(second, (), 0, N_DP, dtype=jnp.int32)
    return jnp.where(jnp.arange(N_DP, dtype=jnp.int32) == full, SEQ, drawn).astype(jnp.int32)


def block_levels(own_key, dims, cuts, low, high):
    factor_of = 1.0
    for dim, parts in cuts:
        heights = jax.random.uniform(jax.random.fold_in(jax.random.fold_in(own_key, 6), dim), (parts,), jnp.float32, low / len(cuts), high / len(cuts))
        factor_of = factor_of * jnp.repeat(jnp.exp(heights), dims[dim] // parts).reshape((-1,) + (1,) * (len(dims) - 1 - dim))
    return factor_of


def scatter_about(stream_key, shape, spread, most, pieces=(), held_as=jnp.bfloat16):
    array = spread * jax.random.normal(stream_key, shape, jnp.float32)
    if pieces:
        array = array * block_levels(stream_key, shape, pieces, -0.22, 0.18)
    return jnp.clip(array, -most, most).astype(held_as)


def setup_inputs(seed: int = 0) -> dict:
    splits = jax.random.split(jax.random.key(seed), 7)
    queries = draw_queries(jax.random.fold_in(splits[6], 71), 0)
    keys = draw_keys(jax.random.fold_in(splits[6], 71), 0)
    values = scatter_about(splits[2], (N_DP, SEQ, HD), 1.0, 6.0, ((0, 8), (1, 32)))
    out_grad = scatter_about(splits[3], (N_DP, SEQ, D), 1.0, 6.0, ((0, 8), (1, 32)))
    q_init = scatter_about(splits[4], (RANK, D), D ** -0.5, 0.09375)
    lengths = draw_lengths(jax.random.fold_in(splits[6], 71), 0)
    return dict(queries=queries, keys=keys, values=values, out_grad=out_grad, q_init=q_init, lengths=lengths)


def attend_stream(queries_one, keys_one, values_one, length):
    span = WINDOW + FR_DEV
    blank = jnp.zeros((WINDOW, HD), jnp.bfloat16)
    keys_pad = jnp.concatenate([blank, keys_one], axis=0)
    values_pad = jnp.concatenate([blank, values_one], axis=0)
    scale = 1.0 / HEAD_DIM ** 0.5

    def block(index):
        start = (index * FR_DEV).astype(jnp.int32)
        q_block = lax.dynamic_slice_in_dim(queries_one, start, FR_DEV, 0).astype(jnp.float32).reshape(FR_DEV, HEADS, HEAD_DIM)
        k_block = lax.dynamic_slice_in_dim(keys_pad, start, span, 0).astype(jnp.float32).reshape(span, HEADS, HEAD_DIM)
        v_block = lax.dynamic_slice_in_dim(values_pad, start, span, 0).astype(jnp.float32).reshape(span, HEADS, HEAD_DIM)
        q_pos = start + jnp.arange(FR_DEV, dtype=jnp.int32)
        k_pos = start - WINDOW + jnp.arange(span, dtype=jnp.int32)
        keep = (k_pos[None, :] <= q_pos[:, None]) & (k_pos[None, :] > q_pos[:, None] - WINDOW) & (k_pos[None, :] >= 0)
        score = jnp.einsum('qhe,khe->hqk', q_block, k_block) * scale
        score = jnp.where(keep[None], score, -1e+30)
        top = jnp.max(score, axis=-1, keepdims=True)
        expo = jnp.exp(score - top)
        total = jnp.sum(expo, axis=-1)
        rounded = lax.optimization_barrier(expo.astype(jnp.bfloat16)).astype(jnp.float32)
        summed = jnp.einsum('hqk,khe->qhe', rounded, v_block)
        result = summed / jnp.transpose(total)[:, :, None]
        result = jnp.where((q_pos < length)[:, None, None], result, 0.0)
        return result.reshape(FR_DEV, HD).astype(jnp.bfloat16)
    blocks = lax.map(block, jnp.arange(SEQ // FR_DEV, dtype=jnp.int32))
    return blocks.reshape(SEQ, HD)

def reference(queries, keys, values, out_grad, q_init, lengths):
    attended = lax.map(lambda items: attend_stream(items[0], items[1], items[2], items[3]), (queries, keys, values, lengths))
    flat_att = attended.reshape(N_DP * SEQ, HD)
    flat_grad = out_grad.reshape(N_DP * SEQ, D)
    proj = jnp.dot(flat_grad.astype(jnp.float32), jnp.transpose(q_init).astype(jnp.float32), preferred_element_type=jnp.float32).astype(jnp.bfloat16)
    p_sum = jnp.dot(jnp.transpose(proj).astype(jnp.float32), flat_att.astype(jnp.float32), preferred_element_type=jnp.float32)
    gram = jnp.dot(p_sum.astype(jnp.float32), jnp.transpose(p_sum).astype(jnp.float32), precision=lax.Precision.HIGHEST, preferred_element_type=jnp.float32)
    lower = jnp.linalg.cholesky(gram)
    p_hat = HD ** 0.5 * lax.linalg.triangular_solve(lower, p_sum, left_side=True, lower=True)
    mapped = jnp.dot(flat_att.astype(jnp.float32), jnp.transpose(p_hat.astype(jnp.bfloat16)).astype(jnp.float32), preferred_element_type=jnp.float32).astype(jnp.bfloat16)
    q_new = jnp.dot(jnp.transpose(mapped).astype(jnp.float32), flat_grad.astype(jnp.float32), preferred_element_type=jnp.float32) / (N_DP * SEQ) ** 0.5
    return (p_hat, q_new)
```

```python
import functools

import jax
import jax.numpy as jnp
from jax import lax
from jax.experimental import pallas as pl
from jax.experimental.pallas import tpu as pltpu
from jax.sharding import PartitionSpec as P

HD = 128
FR = 256
HEADS = 16
WIDTH = HEADS * HD
D = 4096
RANK = 64
REACH = 8
GROUPS = 4
PER = HEADS // GROUPS
CH = PER * HD
HALF = CH // 2
LOG2E = 1.4426950408889634
SCALE2 = LOG2E / HD**0.5
LOW = -1e30
MESH = pl.DeviceIdType.MESH
F32 = jnp.float32
BF16 = jnp.bfloat16


def nt(a, b, **kw):
    return lax.dot_general(a, b, (((1,), (1,)), ((), ())), preferred_element_type=F32, **kw)


def nn(a, b, **kw):
    return lax.dot_general(a, b, (((1,), (0,)), ((), ())), preferred_element_type=F32, **kw)


def kernel(
    len_ref, q_ref, k_ref, v_ref, g_ref, qi_ref, phat_ref, qnew_ref,
    qbuf, ebuf, st_out, st_in, f_out, f_in, pj_in, mp_out, mp_in,
    xp, xp_c, xp_xy, xp_z, psum, xq, xq_c, xq_xy, xq_z, qt,
    ss_x, ss_dm, ss_dp, ss_f1, ss_f3, ss_t, ss_sib, rs_slot, rs_h, rs_sib,
    ss_st, rs_st, ss_f, rs_f, ss_p, rs_p, ss_m, rs_m,
    ss_c, rs_c, ss_xy, rs_xy, ss_z, rs_z, ss_ag, rs_ag,
):
    dp = lax.axis_index("dp")
    ctx = lax.axis_index("ctx")
    zlo, y = dp // 4, dp % 4
    x, zh, core = ctx // 8, (ctx // 2) % 4, ctx % 2
    plane = x * 4 + y
    zz = zh * 2 + zlo

    def at_ctx(i):
        return (dp, lax.rem(i + 64, 32))

    def at_plane(p):
        return (zlo * 4 + p % 4, (p // 4) * 8 + zh * 2 + core)

    def at_z(z):
        return ((z % 2) * 4 + y, x * 8 + (z // 2) * 2 + core)

    sibling = (dp, ctx + 1 - 2 * core)
    up = (dp, x * 8 + ((zh + 1) % 4) * 2 + core)
    down = (dp, x * 8 + ((zh + 3) % 4) * 2 + core)
    left = at_ctx(ctx - 8)
    right = at_ctx(ctx + 8)

    def rc(src, dst, ss, rs, device):
        return pltpu.make_async_remote_copy(
            src_ref=src, dst_ref=dst, send_sem=ss, recv_sem=rs, device_id=device, device_id_type=MESH
        )

    bar = pltpu.get_barrier_semaphore()

    def greet_ctx(i, c):
        pl.semaphore_signal(bar, 1, device_id=at_ctx(ctx + i + 1), device_id_type=MESH)
        pl.semaphore_signal(bar, 1, device_id=at_ctx(ctx - i - 1), device_id_type=MESH)
        return c

    lax.fori_loop(0, REACH, greet_ctx, 0)

    def greet_plane(i, c):
        pl.semaphore_signal(bar, 1, device_id=at_plane((plane + i) % 16), device_id_type=MESH)
        return c

    lax.fori_loop(1, 16, greet_plane, 0)

    def greet_z(i, c):
        pl.semaphore_signal(bar, 1, device_id=at_z((zz + i) % 8), device_id_type=MESH)
        return c

    lax.fori_loop(1, 8, greet_z, 0)
    pl.semaphore_wait(bar, 2 * REACH + 15 + 7)

    def cols(g):
        return pl.ds(g * CH, CH)

    def chunk(d, g):
        return qbuf.at[d, :, cols(g)]

    mid = (zh == 1) | (zh == 2)
    part = jnp.where(mid, 0, HALF)

    def half(d, g):
        return qbuf.at[d, :, pl.ds(pl.multiple_of(g * CH + part, HALF), HALF)]

    def c_x(g):
        return rc(q_ref.at[:, cols(g)], chunk(8, g), ss_x.at[g], rs_slot.at[2, g], left)

    def c_dm(g, own):
        src = q_ref.at[:, cols(g)] if own else chunk(8, g)
        return rc(src, chunk(2, g), ss_dm.at[g], rs_slot.at[0, g], down)

    def c_dp(g, own):
        src = q_ref.at[:, cols(g)] if own else chunk(8, g)
        return rc(src, chunk(6, g), ss_dp.at[g], rs_slot.at[1, g], up)

    def c_f1(g):
        slot = jnp.where(zh == 0, 0, 4)
        sem = jnp.where(mid, 0, jnp.where(zh == 0, 2, 1))
        return rc(half(2, g), half(slot, g), ss_f1.at[g], rs_h.at[sem, g], down)

    def c_f3(g):
        slot = jnp.where(zh == 3, 0, 4)
        sem = jnp.where(mid, 0, jnp.where(zh == 3, 2, 1))
        return rc(half(6, g), half(slot, g), ss_f3.at[g], rs_h.at[sem, g], up)

    def beta(d, g):
        return qbuf.at[d, :, pl.ds(g * CH + HALF, HALF)]

    def alpha(d, g):
        return qbuf.at[d, :, pl.ds(g * CH, HALF)]

    def c_t(g):
        far = (dp, lax.rem(ctx + jnp.where(zh == 0, 8, 24), 32))
        return rc(beta(0, g), beta(4, g), ss_t.at[g], rs_h.at[1, g], far)

    def c_sib(k, g):
        if k == 0:
            src, to = q_ref.at[:, cols(g)], 1
        elif k == 4:
            src, to = chunk(8, g), 7
        else:
            src, to = chunk(2 * k, g), 2 * k - 1 + 2 * core
        return rc(src, chunk(to, g), ss_sib.at[k, g], rs_sib.at[(to - 1) // 2, g], sibling)

    def got(dst, rs):
        rc(dst, dst, ss_x.at[0], rs, sibling).wait_recv()

    keep_row = lax.broadcasted_iota(jnp.int32, (FR, FR), 0)
    keep_col = lax.broadcasted_iota(jnp.int32, (FR, FR), 1)

    def unit(src, d, h, mask):
        hs = pl.ds(pl.multiple_of(h * HD, HD), HD)
        qh = q_ref[:, hs] if src is None else qbuf[src, :, hs]
        s = nt(k_ref[:, hs], qh)
        if mask == 0:
            s = jnp.where(keep_row <= keep_col, s, LOW)
        elif mask == 8:
            s = jnp.where(keep_row > keep_col, s, LOW)
        m = jnp.max(s, axis=0, keepdims=True)
        e = jnp.exp2((s - m) * SCALE2)
        ebuf[d * HEADS + h] = e.astype(BF16)
        row = (d * GROUPS + h // PER) * 8 + h % PER
        st_out[pl.ds(row, 1), :] = m
        st_out[pl.ds(row + PER, 1), :] = jnp.sum(e, axis=0, keepdims=True)

    def units(first, count, g):
        def body(i, c):
            d = first + 2 * (i // PER)
            unit(d, d, g * PER + i % PER, None)
            return c

        lax.fori_loop(0, count * PER, body, 0)

    def units_edge(d, lo, hi):
        def body(h, c):
            unit(None if d == 0 else 8, d, h, d)
            return c

        lax.fori_loop(lo, hi, body, 0)

    def on_x(g):
        got(chunk(8, g), rs_slot.at[2, g])

        @pl.when(zh < 3)
        def _():
            c_dp(g, False).start()

        @pl.when(zh == 0)
        def _():
            c_dm(g, False).start()

        @pl.when(core == 0)
        def _():
            c_sib(4, g).start()

    def on_1(g):
        got(chunk(2, g), rs_slot.at[0, g])
        c_f1(g).start()
        c_sib(1, g).start()

    def on_3(g):
        got(chunk(6, g), rs_slot.at[1, g])
        c_f3(g).start()
        c_sib(3, g).start()

    def on_2(g):
        @pl.when((zh == 0) | (zh == 3))
        def _():
            got(beta(0, g), rs_h.at[2, g])
            c_t(g).start()

        got(alpha(4, g), rs_h.at[0, g])
        got(beta(4, g), rs_h.at[1, g])
        c_sib(2, g).start()

    def on_sib(g):
        for k in range(4):
            got(chunk(2 * k + 1, g), rs_sib.at[k, g])

    def st_rows(ref, d, g):
        return ref.at[pl.ds(pl.multiple_of((d * GROUPS + g) * 8, 8), 8), :]

    def c_st(d, g):
        i = d * GROUPS + g
        return rc(st_rows(st_out, d, g), st_rows(st_in, d, g), ss_st.at[i], rs_st.at[i], at_ctx(ctx + d))

    def c_f(d, g):
        i = d * GROUPS + g
        return rc(st_rows(f_out, d, g), st_rows(f_in, d, g), ss_f.at[i], rs_f.at[i], at_ctx(ctx - d))

    def c_p(d):
        return rc(pj_in.at[0], pj_in.at[d], ss_p.at[d], rs_p.at[d], at_ctx(ctx - d))

    def c_m(d):
        return rc(mp_out.at[d], mp_in.at[d], ss_m.at[d], rs_m.at[d], at_ctx(ctx + d))

    def each(lo, hi, do):
        def body(i, c):
            do(i)
            return c

        lax.fori_loop(lo, hi, body, 0)

    def send_stats(g):
        each(1, REACH + 1, lambda d: c_st(d, g).start())

    def make_factors(g):
        each(1, REACH + 1, lambda d: c_st(d, g).wait_recv())
        tops, sums = [], []
        for d in range(REACH + 1):
            rows = (st_out if d == 0 else st_in)[pl.ds((d * GROUPS + g) * 8, 8), :]
            there = ctx >= d
            tops.append(jnp.where(there, rows[:PER], LOW))
            sums.append(jnp.where(there, rows[PER:], 0.0))
        top = functools.reduce(jnp.maximum, tops)
        ws = [jnp.exp2((t - top) * SCALE2) for t in tops]
        total = functools.reduce(jnp.add, [w * s for w, s in zip(ws, sums)])
        pos = ctx * FR + lax.broadcasted_iota(jnp.int32, (PER, FR), 1)
        inv = jnp.where(pos < len_ref[0], 1.0 / total, 0.0)
        for d in range(REACH + 1):
            f = jnp.where(ctx >= d, ws[d] * inv, 0.0)
            (f_in if d == 0 else f_out)[pl.ds((d * GROUPS + g) * 8, 8), :] = jnp.concatenate([f, f], axis=0)
        each(1, REACH + 1, lambda d: c_f(d, g).start())

    def p_heads(g):
        each(1, REACH + 1, lambda d: c_f(d, g).wait_recv())

        def body(i, c):
            h = g * PER + i
            hs = pl.ds(pl.multiple_of(h * HD, HD), HD)
            acc = jnp.zeros((RANK, FR), F32)
            for d in range(REACH + 1):
                f = f_in[pl.ds((d * GROUPS + g) * 8 + i, 1), :]
                pf = (pj_in[d].astype(F32) * f).astype(BF16)
                acc = acc + nt(pf, ebuf[d * HEADS + h])
            xp[:, hs] = nn(acc.astype(BF16), v_ref[:, hs])
            return c

        lax.fori_loop(0, PER, body, 0)

    def reduce_all(a, buf, buf_c, buf_xy, buf_z, out, rows, width, z_split, scale):
        half_w = width // 2
        mine = pl.ds(pl.multiple_of(core * half_w, half_w), half_w)
        other = pl.ds(pl.multiple_of((1 - core) * half_w, half_w), half_w)
        per_col = RANK // rows
        cc = rc(buf.at[:, other], buf_c, ss_c.at[2 * a], rs_c.at[2 * a], sibling)
        cc.start()
        cc.wait_recv()

        def add(i, c):
            s = pl.ds(pl.multiple_of(i * 128, 128), 128)
            t = pl.ds(pl.multiple_of(core * half_w + i * 128, 128), 128)
            buf_c[:, s] = buf_c[:, s] + buf[:, t]
            return c

        lax.fori_loop(0, half_w // 128, add, 0)

        def piece(ref, p, base):
            r = pl.ds(pl.multiple_of((p % per_col) * rows, rows), rows)
            c = pl.ds(pl.multiple_of(base + (p // per_col) * 128, 128), 128)
            return ref.at[r, c]

        def c_xy(k):
            p = (plane + k) % 16
            return rc(piece(buf_c, p, 0), buf_xy.at[plane], ss_xy.at[a, k], rs_xy.at[a, plane], at_plane(p))

        def got_xy(k):
            p = (plane + k) % 16
            got(buf_xy.at[p], rs_xy.at[a, p])

        each(1, 16, lambda k: c_xy(k).start())
        buf_xy[plane] = piece(buf_c, plane, 0)[...]
        each(1, 16, got_xy)
        part_sum = buf_xy[0]
        for p in range(1, 16):
            part_sum = part_sum + buf_xy[p]
        if z_split:
            buf_xy[0] = part_sum
            zr = rows // 8

            def c_z(k):
                z = (zz + k) % 8
                src = buf_xy.at[0, pl.ds(pl.multiple_of(z * zr, zr), zr), :]
                return rc(src, buf_z.at[zz], ss_z.at[a, k], rs_z.at[a, zz], at_z(z))

            def got_z(k):
                z = (zz + k) % 8
                got(buf_z.at[z], rs_z.at[a, z])

            each(1, 8, lambda k: c_z(k).start())
            buf_z[zz] = buf_xy[0, pl.ds(pl.multiple_of(zz * zr, zr), zr), :]
            each(1, 8, got_z)
            total = buf_z[0]
            for z in range(1, 8):
                total = total + buf_z[z]
            home = piece(out, plane, core * half_w)
            r0 = (plane % per_col) * rows
            c0 = pl.ds(pl.multiple_of(core * half_w + (plane // per_col) * 128, 128), 128)

            def line(z):
                return out.at[pl.ds(pl.multiple_of(r0 + z * zr, zr), zr), c0]

            out[pl.ds(pl.multiple_of(r0 + zz * zr, zr), zr), c0] = total * scale

            def c_z2(k):
                return rc(line(zz), line(zz), ss_z.at[2, k], rs_z.at[2, zz], at_z((zz + k) % 8))

            each(1, 8, lambda k: c_z2(k).start())

            def got_z2(k):
                z = (zz + k) % 8
                got(line(z), rs_z.at[2, z])

            each(1, 8, got_z2)
        else:
            buf_z[zz] = part_sum

            def c_z(k):
                return rc(buf_z.at[zz], buf_z.at[zz], ss_z.at[a, k], rs_z.at[a, zz], at_z((zz + k) % 8))

            each(1, 8, lambda k: c_z(k).start())

            def got_z(k):
                z = (zz + k) % 8
                got(buf_z.at[z], rs_z.at[a, z])

            each(1, 8, got_z)
            total = buf_z[0]
            for z in range(1, 8):
                total = total + buf_z[z]
            r0 = pl.ds(pl.multiple_of((plane % per_col) * rows, rows), rows)
            c0 = pl.ds(pl.multiple_of(core * half_w + (plane // per_col) * 128, 128), 128)
            out[r0, c0] = total * scale

        def c_ag(k):
            ref = piece(out, plane, core * half_w)
            return rc(ref, ref, ss_ag.at[a, k], rs_ag.at[a, plane], at_plane((plane + k) % 16))

        def got_ag(k):
            p = (plane + k) % 16
            got(piece(out, p, core * half_w), rs_ag.at[a, p])

        each(1, 16, lambda k: c_ag(k).start())
        each(1, 16, got_ag)
        c2 = rc(out.at[:, mine], out.at[:, mine], ss_c.at[2 * a + 1], rs_c.at[2 * a + 1], sibling)
        c2.start()
        got(out.at[:, other], rs_c.at[2 * a + 1])
        cc.wait_send()
        c2.wait_send()
        each(1, 16, lambda k: c_xy(k).wait_send())
        each(1, 16, lambda k: c_ag(k).wait_send())
        each(1, 8, lambda k: c_z(k).wait_send())
        if z_split:
            each(1, 8, lambda k: c_z2(k).wait_send())

    for g in range(GROUPS):
        c_x(g).start()

        @pl.when(zh > 0)
        def _():
            c_dm(g, True).start()

        @pl.when(zh == 3)
        def _():
            c_dp(g, True).start()

        @pl.when(core == 1)
        def _():
            c_sib(0, g).start()

    pj_in[0] = nt(qi_ref[...], g_ref[...]).astype(BF16)
    each(1, REACH + 1, lambda d: c_p(d).start())
    units_edge(0, 0, HEADS)
    on_x(0)
    on_x(1)
    on_1(0)
    on_x(2)
    on_3(0)
    on_x(3)
    units_edge(8, 0, HEADS)
    units(2, 1, 0)
    units(6, 1, 0)
    for g in range(1, GROUPS):
        on_1(g)
        units(2, 1, g)
        on_3(g)
        units(6, 1, g)
        on_2(g - 1)
        on_sib(g - 1)
        units(1, 4, g - 1)
        units(4, 1, g - 1)
        send_stats(g - 1)
        if g > 1:
            make_factors(g - 2)
        if g == 2:
            each(1, REACH + 1, lambda d: c_p(d).wait_recv())
        if g > 2:
            p_heads(g - 3)
    last = GROUPS - 1
    on_2(last)
    units(4, 1, last)
    on_sib(last)
    units(1, 4, last)
    send_stats(last)
    make_factors(last - 1)
    p_heads(last - 2)
    make_factors(last)
    p_heads(last - 1)
    p_heads(last)

    reduce_all(0, xp, xp_c, xp_xy, xp_z, psum, 32, WIDTH, False, 1.0)

    p_sum = psum[...]
    gram = nt(p_sum, p_sum, precision=lax.Precision.HIGHEST)
    row_i = lax.broadcasted_iota(jnp.int32, (RANK, 2 * RANK), 0)
    col_i = lax.broadcasted_iota(jnp.int32, (RANK, 2 * RANK), 1)
    a = jnp.concatenate([gram, jnp.zeros((RANK, RANK), F32)], axis=1)
    a = jnp.where(col_i == row_i + RANK, 1.0, a)
    pivots = jnp.zeros((RANK, 2 * RANK), F32)
    for k in range(RANK):
        wide = jnp.broadcast_to(a[:, k : k + 1], (RANK, 2 * RANK))
        piv = wide[k : k + 1, :]
        line = a[k : k + 1, :] / piv
        pivots = jnp.where(row_i == k, piv, pivots)
        a = a - jnp.where(row_i > k, wide, 0.0) * line
    inv_low = a[:, RANK:] * (lax.rsqrt(pivots[:, RANK:]) * (WIDTH**0.5))
    phat_ref[...] = nn(inv_low, p_sum, precision=lax.Precision.HIGHEST)

    def values_in(h, c):
        hs = pl.ds(pl.multiple_of(h * HD, HD), HD)
        pj_in[pl.ds(REACH + 1 + h, 1)] = nt(phat_ref[:, hs].astype(BF16), v_ref[:, hs]).astype(BF16)[None]
        return c

    lax.fori_loop(0, HEADS, values_in, 0)

    def mapped_of(i, c):
        d = REACH - i

        def head(h, acc):
            f = f_in[pl.ds((d * GROUPS + h // PER) * 8 + h % PER, 1), :]
            return acc + nn(pj_in[REACH + 1 + h], ebuf[d * HEADS + h]) * f

        acc = lax.fori_loop(0, HEADS, head, jnp.zeros((RANK, FR), F32))
        mp_out[pl.ds(d, 1)] = acc.astype(BF16)[None]

        @pl.when(d > 0)
        def _():
            c_m(d).start()

        return c

    lax.fori_loop(0, REACH + 1, mapped_of, 0)
    acc = mp_out[0].astype(F32)
    for d in range(1, REACH + 1):
        c_m(d).wait_recv()
        acc = acc + jnp.where(ctx >= d, mp_in[d].astype(F32), 0.0)
    mapped = acc.astype(BF16)

    def q_cols(i, c):
        s = pl.ds(pl.multiple_of(i * 512, 512), 512)
        xq[:, s] = nn(mapped, g_ref[:, s])
        return c

    lax.fori_loop(0, D // 512, q_cols, 0)
    reduce_all(1, xq, xq_c, xq_xy, xq_z, qt, RANK, D, True, 1.0 / 256.0)
    qnew_ref[...] = qt[...]

    for g in range(GROUPS):
        c_x(g).wait_send()
        c_dm(g, True).wait_send()
        c_dp(g, True).wait_send()
        c_f1(g).wait_send()
        c_f3(g).wait_send()
        for k in (1, 2, 3):
            c_sib(k, g).wait_send()

        @pl.when((zh == 0) | (zh == 3))
        def _():
            c_t(g).wait_send()

        @pl.when(core == 1)
        def _():
            c_sib(0, g).wait_send()

        @pl.when(core == 0)
        def _():
            c_sib(4, g).wait_send()

        each(1, REACH + 1, lambda d: c_st(d, g).wait_send())
        each(1, REACH + 1, lambda d: c_f(d, g).wait_send())
    each(1, REACH + 1, lambda d: c_p(d).wait_send())
    each(1, REACH + 1, lambda d: c_m(d).wait_send())


def local(queries, keys, values, out_grad, q_init, lengths):
    dma = pltpu.SemaphoreType.DMA
    n = REACH + 1
    vm = pl.BlockSpec(memory_space=pltpu.VMEM)
    p_hat, q_new = pl.pallas_call(
        kernel,
        out_shape=(
            jax.ShapeDtypeStruct((RANK, WIDTH), F32),
            jax.ShapeDtypeStruct((RANK, D), F32),
        ),
        in_specs=[pl.BlockSpec(memory_space=pltpu.SMEM)] + [vm] * 5,
        out_specs=(vm, vm),
        scratch_shapes=[
            pltpu.VMEM((n, FR, WIDTH), BF16),
            pltpu.VMEM((n * HEADS, FR, FR), BF16),
            pltpu.VMEM((n * GROUPS * 8, FR), F32),
            pltpu.VMEM((n * GROUPS * 8, FR), F32),
            pltpu.VMEM((n * GROUPS * 8, FR), F32),
            pltpu.VMEM((n * GROUPS * 8, FR), F32),
            pltpu.VMEM((n + HEADS, RANK, FR), BF16),
            pltpu.VMEM((n, RANK, FR), BF16),
            pltpu.VMEM((n, RANK, FR), BF16),
            pltpu.VMEM((RANK, WIDTH), F32),
            pltpu.VMEM((RANK, WIDTH // 2), F32),
            pltpu.VMEM((16, 32, 128), F32),
            pltpu.VMEM((8, 32, 128), F32),
            pltpu.VMEM((RANK, WIDTH), F32),
            pltpu.VMEM((RANK, D), F32),
            pltpu.VMEM((RANK, D // 2), F32),
            pltpu.VMEM((16, RANK, 128), F32),
            pltpu.VMEM((8, 8, 128), F32),
            pltpu.VMEM((RANK, D), F32),
            dma((4,)), dma((4,)), dma((4,)), dma((4,)), dma((4,)), dma((4,)), dma((5, 4)),
            dma((3, 4)), dma((3, 4)), dma((4, 4)),
            dma((n * GROUPS,)), dma((n * GROUPS,)), dma((n * GROUPS,)), dma((n * GROUPS,)),
            dma((n,)), dma((n,)), dma((n,)), dma((n,)),
            dma((4,)), dma((4,)), dma((2, 16)), dma((2, 16)), dma((3, 8)), dma((3, 8)),
            dma((2, 16)), dma((2, 16)),
        ],
        compiler_params=pltpu.CompilerParams(
            collective_id=0, has_side_effects=True, vmem_limit_bytes=60 << 20
        ),
        name="attend",
    )(lengths, queries[0], keys[0], values[0], out_grad[0], q_init)
    return (p_hat, q_new)


def solution(mesh):
    placed = (
        P("dp", "ctx", None),
        P("dp", "ctx", None),
        P("dp", "ctx", None),
        P("dp", "ctx", None),
        P(),
        P("dp"),
    )
    return jax.shard_map(local, mesh=mesh, in_specs=placed, out_specs=(P(), P()), check_vma=False)
```

```python
import functools

import jax
import jax.numpy as jnp
from jax import lax
from jax.experimental import pallas as pl
from jax.experimental.pallas import tpu as pltpu
from jax.sharding import PartitionSpec as P

HD = 128
FR = 256
HEADS = 16
WIDTH = HEADS * HD
D = 4096
RANK = 64
REACH = 8
GROUPS = 4
PER = HEADS // GROUPS
PARTS = GROUPS
CH = WIDTH // PARTS
LOG2E = 1.4426950408889634
SCALE2 = LOG2E / HD**0.5
LOW = -1e30
MESH = pl.DeviceIdType.MESH
F32 = jnp.float32
BF16 = jnp.bfloat16


def nt(a, b, **kw):
    return lax.dot_general(a, b, (((1,), (1,)), ((), ())), preferred_element_type=F32, **kw)


def nn(a, b, **kw):
    return lax.dot_general(a, b, (((1,), (0,)), ((), ())), preferred_element_type=F32, **kw)


def kernel(
    len_ref, q_any, k_any, v_any, g_any, qi_any, phat_ref, qnew_ref,
    q_ref, k_ref, v_ref, g_ref, qi_ref,
    qbuf, ebuf, mx, lg_out, lg_in, ls_out, ls_in, fac, pj_in, yacc, mp_out, mp_in,
    xp, xr, xz, psum, xq, xq_c, xq_b, xq_xy, xq_z, qg,
    ss_in, ss_x, ss_dm, ss_dp, ss_f1, ss_f3, ss_t, ss_sib, rs_slot, rs_h, rs_sib,
    ss_g, rs_g, ss_o, rs_o, ss_q, rs_q,
):
    dp = lax.axis_index("dp")
    ctx = lax.axis_index("ctx")
    zlo, y = dp // 4, dp % 4
    x, zh, core = ctx // 8, (ctx // 2) % 4, ctx % 2
    plane = x * 4 + y
    zz = zh * 2 + zlo
    rank = plane * 2 + core

    def at_ctx(i):
        return (dp, lax.rem(i + 64, 32))

    def at_plane(p):
        return (zlo * 4 + p % 4, (p // 4) * 8 + zh * 2 + core)

    def at_rank(r):
        return (zlo * 4 + (r // 2) % 4, (r // 8) * 8 + zh * 2 + r % 2)

    def at_z(z):
        return ((z % 2) * 4 + y, x * 8 + (z // 2) * 2 + core)

    sibling = (dp, ctx + 1 - 2 * core)
    up = (dp, x * 8 + ((zh + 1) % 4) * 2 + core)
    down = (dp, x * 8 + ((zh + 3) % 4) * 2 + core)
    left = at_ctx(ctx - 8)

    def rc(src, dst, ss, rs, device):
        return pltpu.make_async_remote_copy(
            src_ref=src, dst_ref=dst, send_sem=ss, recv_sem=rs, device_id=device, device_id_type=MESH
        )

    def each(lo, hi, do):
        def body(i, c):
            do(i)
            return c

        lax.fori_loop(lo, hi, body, 0)

    loads = [
        pltpu.make_async_copy(a, b, ss_in.at[i])
        for i, (a, b) in enumerate(
            ((q_any, q_ref), (k_any, k_ref), (g_any, g_ref), (qi_any, qi_ref), (v_any, v_ref))
        )
    ]
    for load in loads:
        load.start()

    bar = pltpu.get_barrier_semaphore()

    def greet(device):
        pl.semaphore_signal(bar, 1, device_id=device, device_id_type=MESH)

    def greet_ctx(i):
        greet(at_ctx(ctx + i))
        greet(at_ctx(ctx - i))

    each(1, REACH + 1, greet_ctx)
    each(1, 32, lambda i: greet(at_rank((rank + i) % 32)))
    each(1, 8, lambda i: greet(at_z((zz + i) % 8)))
    pl.semaphore_wait(bar, 2 * REACH + 31 + 7)

    def cols(g):
        return pl.ds(g * CH, CH)

    def chunk(d, g):
        return qbuf.at[d, :, cols(g)]

    mid = (zh == 1) | (zh == 2)
    edge = (zh == 0) | (zh == 3)

    def c_x(g):
        return rc(q_ref.at[:, cols(g)], chunk(8, g), ss_x.at[g], rs_slot.at[2, g], left)

    def c_dm(g, own):
        src = q_ref.at[:, cols(g)] if own else chunk(8, g)
        return rc(src, chunk(2, g), ss_dm.at[g], rs_slot.at[0, g], down)

    def c_dp(g, own):
        src = q_ref.at[:, cols(g)] if own else chunk(8, g)
        return rc(src, chunk(6, g), ss_dp.at[g], rs_slot.at[1, g], up)

    def c_f1(g):
        slot, sem = jnp.where(zh == 0, 0, 4), jnp.where(zh == 0, 1, 0)
        return rc(chunk(2, g), chunk(slot, g), ss_f1.at[g], rs_h.at[sem, g], down)

    def c_f3(g):
        slot, sem = jnp.where(zh == 3, 0, 4), jnp.where(zh == 3, 1, 0)
        return rc(chunk(6, g), chunk(slot, g), ss_f3.at[g], rs_h.at[sem, g], up)

    def forwards(g):
        return edge if g < PARTS // 2 else mid

    def c_t(g):
        far = (dp, lax.rem(ctx + jnp.where(zh == 0, 8, 24), 32))
        return rc(chunk(0, g), chunk(4, g), ss_t.at[g], rs_h.at[0, g], far)

    def c_sib(k, g):
        if k == 0:
            src, to = q_ref.at[:, cols(g)], 1
        elif k == 4:
            src, to = chunk(8, g), 7
        else:
            src, to = chunk(2 * k, g), 2 * k - 1 + 2 * core
        return rc(src, chunk(to, g), ss_sib.at[k, g], rs_sib.at[(to - 1) // 2, g], sibling)

    def got(dst, rs):
        rc(dst, dst, ss_x.at[0], rs, sibling).wait_recv()

    def left_all(src, ss):
        rc(src, src, ss, rs_g.at[0, 0], sibling).wait_send()

    keep_row = lax.broadcasted_iota(jnp.int32, (FR, FR), 0)
    keep_col = lax.broadcasted_iota(jnp.int32, (FR, FR), 1)

    def fold(a):
        return jnp.concatenate([a[:, : FR // 2], a[:, FR // 2 :]], axis=0)

    def unfold(a):
        return jnp.concatenate([a[:PER], a[PER:]], axis=1)

    def stat(ref, d, g):
        return ref.at[pl.ds(pl.multiple_of((d * GROUPS + g) * 8, 8), 8), :]

    def unit(d, g):
        tops, sums = [], []
        for i in range(PER):
            h = g * PER + i
            hs = slice(h * HD, h * HD + HD)
            qh = q_ref[:, hs] if isinstance(d, int) and d == 0 else qbuf[d, :, hs]
            s = nt(k_ref[:, hs], qh)
            if isinstance(d, int) and d == 0:
                s = jnp.where(keep_row <= keep_col, s, LOW)
            elif isinstance(d, int) and d == 8:
                s = jnp.where(keep_row > keep_col, s, LOW)
            m = jnp.max(s, axis=0, keepdims=True)
            e = jnp.exp2((s - m) * SCALE2)
            ebuf[d * HEADS + h] = e.astype(BF16)
            tops.append(m)
            sums.append(jnp.sum(e, axis=0, keepdims=True))
        top = jnp.concatenate(tops, axis=0) * SCALE2
        logs = top + jnp.log2(jnp.concatenate(sums, axis=0))
        stat(mx, d, g)[...] = jnp.concatenate([top, top], axis=0)
        lg_out[g, d] = fold(logs)

    def odd_units(g):
        each(0, 4, lambda i: unit(1 + 2 * i, g))

    def on_x(g):
        got(chunk(8, g), rs_slot.at[2, g])

        @pl.when(core == 0)
        def _():
            c_sib(4, g).start()

    def on_1(g):
        got(chunk(2, g), rs_slot.at[0, g])
        pl.when(forwards(g))(lambda: c_f1(g).start())
        c_sib(1, g).start()

    def on_3(g):
        got(chunk(6, g), rs_slot.at[1, g])
        pl.when(forwards(g))(lambda: c_f3(g).start())
        c_sib(3, g).start()

    def on_t(g):
        @pl.when(edge)
        def _():
            got(chunk(0, g), rs_h.at[1, g])
            c_t(g).start()

    def on_2(g):
        got(chunk(4, g), rs_h.at[0, g])
        c_sib(2, g).start()

    def on_sib(g):
        for k in range(4):
            got(chunk(2 * k + 1, g), rs_sib.at[k, g])

    def c_lg(d, g):
        return rc(lg_out.at[g, d], lg_in.at[g, d], ss_g.at[0, g], rs_g.at[0, g], at_ctx(ctx + d))

    def c_ls(d, g):
        return rc(ls_out.at[g], ls_in.at[g, d], ss_g.at[1, g], rs_g.at[1, g], at_ctx(ctx - d))

    def c_p(k):
        return rc(pj_in.at[0], pj_in.at[2 * k], ss_o.at[0], rs_o.at[0], at_ctx(ctx - 2 * k))

    def c_ps(k):
        src, to = (pj_in.at[0], 1) if k == 0 else (pj_in.at[2 * k], 2 * k - 1 + 2 * core)
        if k == 4:
            to = 7
        return rc(src, pj_in.at[to], ss_o.at[2], rs_o.at[2], sibling)

    def share_proj():
        got(pj_in.at[pl.ds(1, 4)], rs_o.at[0])
        for k in (1, 2, 3):
            c_ps(k).start()

        @pl.when(core == 0)
        def _():
            c_ps(4).start()

        @pl.when(core == 1)
        def _():
            c_ps(0).start()

    def c_m(d):
        return rc(mp_out.at[d], mp_in.at[d], ss_o.at[1], rs_o.at[1], at_ctx(ctx + d))

    def stage_a(g):
        each(1, REACH + 1, lambda d: c_lg(d, g).start())

    def stage_b(g):
        got(lg_in.at[g, pl.ds(1, REACH)], rs_g.at[0, g])
        logs = [lg_out[g, 0]]
        for d in range(1, REACH + 1):
            logs.append(jnp.where(ctx >= d, lg_in[g, d], LOW))
        top = functools.reduce(jnp.maximum, logs)
        total = functools.reduce(jnp.add, [jnp.exp2(a - top) for a in logs])
        ls_out[g] = top + jnp.log2(total)
        each(1, REACH + 1, lambda d: c_ls(d, g).start())

    def c_rs(k, g):
        r = (rank + k) % 32
        return rc(xp.at[g, r], xr.at[g, rank], ss_g.at[2, g], rs_g.at[2, g], at_rank(r))

    def c_z(k, g):
        return rc(xz.at[g, zz], xz.at[g, zz], ss_g.at[3, g], rs_g.at[3, g], at_z((zz + k) % 8))

    def c_ag(k, g):
        ref = psum.at[g, rank]
        return rc(ref, ref, ss_g.at[4, g], rs_g.at[4, g], at_rank((rank + k) % 32))

    def stage_c(g):
        got(ls_in.at[g, pl.ds(1, REACH)], rs_g.at[1, g])
        lane = lax.broadcasted_iota(jnp.int32, (PER, FR), 1)
        accs = [jnp.zeros((RANK, FR), F32) for _ in range(PER)]
        for d in range(REACH + 1):
            ls = unfold(ls_out[g] if d == 0 else ls_in[g, d])
            pos = (ctx + d) * FR + lane
            f = jnp.exp2(stat(mx, d, g)[...][:PER] - ls)
            f = jnp.where((pos < len_ref[0]) & (ctx + d < 32), f, 0.0)
            stat(fac, d, g)[...] = jnp.concatenate([f, f], axis=0)
            pj = pj_in[d].astype(F32)
            for i in range(PER):
                pf = (pj * f[i : i + 1, :]).astype(BF16)
                accs[i] = accs[i] + nt(pf, ebuf[d * HEADS + g * PER + i])
        for i in range(PER):
            hs = slice((g * PER + i) * HD, (g * PER + i + 1) * HD)
            xp[g, 8 * i : 8 * i + 8] = nn(accs[i].astype(BF16), v_ref[:, hs]).reshape(8, 8, HD)
        each(1, 32, lambda k: c_rs(k, g).start())

    def stage_f(g):
        xr[g, rank] = xp[g, rank]
        got(xr.at[g, pl.ds(0, 31)], rs_g.at[2, g])
        total = xr[g, 0]
        for r in range(1, 32):
            total = total + xr[g, r]
        xz[g, zz] = total
        each(1, 8, lambda k: c_z(k, g).start())

    def stage_g(g):
        got(xz.at[g, pl.ds(0, 7)], rs_g.at[3, g])
        total = xz[g, 0]
        for z in range(1, 8):
            total = total + xz[g, z]
        psum[g, rank] = total
        each(1, 32, lambda k: c_ag(k, g).start())

    def p_head(g, i):
        return psum[g, 8 * i : 8 * i + 8].reshape(RANK, HD)

    def stage_i(g):
        got(psum.at[g, pl.ds(0, 31)], rs_g.at[4, g])
        us = []
        for i in range(PER):
            hs = slice((g * PER + i) * HD, (g * PER + i + 1) * HD)
            us.append(nt(p_head(g, i).astype(BF16), v_ref[:, hs]).astype(BF16))

        def part_of(d, start):
            f = stat(fac, d, g)[...]
            acc = start
            for i in range(PER):
                acc = acc + nn(us[i], ebuf[d * HEADS + g * PER + i]) * f[i : i + 1, :]
            return acc

        for i in range(REACH + 1):
            d = REACH - i
            acc = part_of(d, jnp.zeros((RANK, FR), F32) if g == 0 else yacc[d])
            if g < GROUPS - 1 or d == 0:
                yacc[d] = acc
            else:
                mp_out[d] = acc.astype(BF16)
                c_m(d).start()

    loads[0].wait()
    for g in range(PARTS):
        c_x(g).start()

        @pl.when(core == 1)
        def _():
            c_sib(0, g).start()

    early = PARTS // 2

    def own_down(g):
        pl.when(zh > 0)(lambda: c_dm(g, True).start())

    def own_up(g):
        pl.when(zh == 3)(lambda: c_dp(g, True).start())

    for g in range(PARTS):
        own_down(g)
        if g < early:
            own_up(g)

    def pass_on(g):
        if g < early:
            pl.when(zh == 0)(lambda: c_dm(g, False).start())
        pl.when(zh < 3)(lambda: c_dp(g, False).start())

    def late_down():
        for g in range(early, PARTS):
            pl.when(zh == 0)(lambda: c_dm(g, False).start())

    def late_up():
        for g in range(early, PARTS):
            own_up(g)

    for load in loads[1:4]:
        load.wait()
    pj_in[0] = nt(qi_ref[...], g_ref[...]).astype(BF16)
    each(1, 5, lambda k: c_p(k).start())
    loads[4].wait()
    on_x(0)
    pass_on(0)
    unit(0, 0)
    unit(8, 0)
    on_x(1)
    pass_on(1)
    unit(0, 1)
    unit(8, 1)
    on_1(0)
    on_x(2)
    pass_on(2)
    on_3(0)
    on_x(3)
    pass_on(3)
    on_1(1)
    late_down()
    on_3(1)
    late_up()
    unit(0, 2)
    unit(8, 2)
    unit(0, 3)
    unit(8, 3)
    unit(2, 0)
    unit(6, 0)
    unit(2, 1)
    unit(6, 1)
    on_t(0)
    on_1(2)
    on_3(2)
    unit(2, 2)
    unit(6, 2)
    on_t(1)
    on_1(3)
    on_3(3)
    unit(2, 3)
    unit(6, 3)

    def complete(g):
        on_2(g)
        unit(4, g)
        on_sib(g)
        odd_units(g)
        stage_a(g)

    complete(0)
    share_proj()
    complete(2)
    got(pj_in.at[pl.ds(1, 4)], rs_o.at[2])
    stage_b(0)
    complete(1)
    stage_b(2)
    stage_c(0)
    complete(3)
    stage_b(1)
    stage_c(2)
    stage_b(3)
    stage_c(1)
    stage_f(0)
    stage_f(2)
    stage_c(3)
    stage_f(1)
    stage_g(0)
    stage_g(2)
    stage_f(3)
    stage_g(1)
    stage_g(3)
    stage_i(0)
    stage_i(1)
    stage_i(2)
    stage_i(3)

    p_sum = jnp.concatenate([p_head(g, i) for g in range(GROUPS) for i in range(PER)], axis=1)
    gram = nt(p_sum, p_sum, precision=lax.Precision.HIGHEST)
    row_i = lax.broadcasted_iota(jnp.int32, (RANK, 2 * RANK), 0)
    col_i = lax.broadcasted_iota(jnp.int32, (RANK, 2 * RANK), 1)
    a = jnp.concatenate([gram, jnp.zeros((RANK, RANK), F32)], axis=1)
    a = jnp.where(col_i == row_i + RANK, 1.0, a)
    pivots = jnp.zeros((RANK, 2 * RANK), F32)
    for k in range(RANK):
        wide = jnp.broadcast_to(a[:, k : k + 1], (RANK, 2 * RANK))
        piv = wide[k : k + 1, :]
        line = a[k : k + 1, :] / piv
        pivots = jnp.where(row_i == k, piv, pivots)
        a = a - jnp.where(row_i > k, wide, 0.0) * line
    inv_low = a[:, RANK:] * (lax.rsqrt(pivots[:, RANK:]) * (WIDTH**0.5))

    got(mp_in.at[pl.ds(1, REACH)], rs_o.at[1])
    acc = yacc[0]
    for d in range(1, REACH + 1):
        acc = acc + jnp.where(ctx >= d, mp_in[d].astype(F32), 0.0)
    mapped = nn(inv_low, acc, precision=lax.Precision.HIGHEST).astype(BF16)

    half_w = D // 2
    mine = pl.ds(pl.multiple_of(core * half_w, half_w), half_w)
    other = pl.ds(pl.multiple_of((1 - core) * half_w, half_w), half_w)
    step = 512

    def q_cols(base, i):
        s = pl.ds(pl.multiple_of(base + i * step, step), step)
        xq[:, s] = nn(mapped, g_ref[:, s])

    each(0, half_w // step, lambda i: q_cols((1 - core) * half_w, i))
    cc = rc(xq.at[:, other], xq_c, ss_q.at[0], rs_q.at[0], sibling)
    cc.start()
    each(0, half_w // step, lambda i: q_cols(core * half_w, i))
    cc.wait_recv()

    def join(i):
        s = pl.ds(pl.multiple_of(i * 128, 128), 128)
        t = pl.ds(pl.multiple_of(core * half_w + i * 128, 128), 128)
        xq_b[i] = (xq_c[:, s] + xq[:, t]).astype(BF16)

    each(0, 16, join)

    def c_qx(k):
        p = (plane + k) % 16
        return rc(xq_b.at[p], xq_xy.at[plane], ss_q.at[1], rs_q.at[1], at_plane(p))

    each(1, 16, lambda k: c_qx(k).start())
    xq_xy[plane] = xq_b[plane]
    got(xq_xy.at[pl.ds(0, 15)], rs_q.at[1])
    total = xq_xy[0].astype(F32)
    for p in range(1, 16):
        total = total + xq_xy[p].astype(F32)
    xq_z[zz] = total.astype(BF16)

    def c_qz(k):
        return rc(xq_z.at[zz], xq_z.at[zz], ss_q.at[2], rs_q.at[2], at_z((zz + k) % 8))

    each(1, 8, lambda k: c_qz(k).start())
    phat_ref[...] = nn(inv_low, p_sum, precision=lax.Precision.HIGHEST)
    got(xq_z.at[pl.ds(0, 7)], rs_q.at[2])
    total = xq_z[0].astype(F32)
    for z in range(1, 8):
        total = total + xq_z[z].astype(F32)
    done = total * (1.0 / 256.0)
    qg[core, plane] = done.astype(BF16)

    def c_qa(k):
        ref = qg.at[core, plane]
        return rc(ref, ref, ss_q.at[3], rs_q.at[3], at_plane((plane + k) % 16))

    each(1, 16, lambda k: c_qa(k).start())
    got(qg.at[core, pl.ds(0, 15)], rs_q.at[3])
    c2 = rc(qg.at[core], qg.at[core], ss_q.at[4], rs_q.at[4], sibling)
    c2.start()
    got(qg.at[1 - core], rs_q.at[4])
    for i in range(32):
        qnew_ref[:, i * 128 : i * 128 + 128] = qg[i // 16, i % 16].astype(F32)

    for g in range(PARTS):
        c_x(g).wait_send()
        c_dm(g, True).wait_send()
        c_dp(g, True).wait_send()

        @pl.when(forwards(g))
        def _():
            c_f1(g).wait_send()
            c_f3(g).wait_send()

        for k in (1, 2, 3):
            c_sib(k, g).wait_send()

        if g < PARTS // 2:

            @pl.when(edge)
            def _():
                c_t(g).wait_send()

        @pl.when(core == 1)
        def _():
            c_sib(0, g).wait_send()

        @pl.when(core == 0)
        def _():
            c_sib(4, g).wait_send()

    for g in range(GROUPS):
        left_all(lg_in.at[g, pl.ds(0, REACH)], ss_g.at[0, g])
        left_all(ls_in.at[g, pl.ds(0, REACH)], ss_g.at[1, g])
        left_all(xr.at[g, pl.ds(0, 31)], ss_g.at[2, g])
        left_all(xz.at[g, pl.ds(0, 7)], ss_g.at[3, g])
        left_all(psum.at[g, pl.ds(0, 31)], ss_g.at[4, g])
    left_all(pj_in.at[pl.ds(0, 4)], ss_o.at[0])
    left_all(pj_in.at[pl.ds(0, 4)], ss_o.at[2])
    left_all(mp_in.at[pl.ds(0, REACH)], ss_o.at[1])
    cc.wait_send()
    left_all(xq_xy.at[pl.ds(0, 15)], ss_q.at[1])
    left_all(xq_z.at[pl.ds(0, 7)], ss_q.at[2])
    left_all(qg.at[core, pl.ds(0, 15)], ss_q.at[3])
    c2.wait_send()


def local(queries, keys, values, out_grad, q_init, lengths):
    dma = pltpu.SemaphoreType.DMA
    n = REACH + 1
    vm = pl.BlockSpec(memory_space=pltpu.VMEM)
    p_hat, q_new = pl.pallas_call(
        kernel,
        out_shape=(
            jax.ShapeDtypeStruct((RANK, WIDTH), F32),
            jax.ShapeDtypeStruct((RANK, D), F32),
        ),
        in_specs=[pl.BlockSpec(memory_space=pltpu.SMEM)] + [pl.BlockSpec(memory_space=pl.ANY)] * 5,
        out_specs=(vm, vm),
        scratch_shapes=[
            pltpu.VMEM((FR, WIDTH), BF16),
            pltpu.VMEM((FR, WIDTH), BF16),
            pltpu.VMEM((FR, WIDTH), BF16),
            pltpu.VMEM((FR, D), BF16),
            pltpu.VMEM((RANK, D), BF16),
            pltpu.VMEM((n, FR, WIDTH), BF16),
            pltpu.VMEM((n * HEADS, FR, FR), BF16),
            pltpu.VMEM((n * GROUPS * 8, FR), F32),
            pltpu.VMEM((GROUPS, n, 8, 128), F32),
            pltpu.VMEM((GROUPS, n, 8, 128), F32),
            pltpu.VMEM((GROUPS, 8, 128), F32),
            pltpu.VMEM((GROUPS, n, 8, 128), F32),
            pltpu.VMEM((n * GROUPS * 8, FR), F32),
            pltpu.VMEM((n, RANK, FR), BF16),
            pltpu.VMEM((n, RANK, FR), F32),
            pltpu.VMEM((n, RANK, FR), BF16),
            pltpu.VMEM((n, RANK, FR), BF16),
            pltpu.VMEM((GROUPS, 32, 8, 128), F32),
            pltpu.VMEM((GROUPS, 32, 8, 128), F32),
            pltpu.VMEM((GROUPS, 8, 8, 128), F32),
            pltpu.VMEM((GROUPS, 32, 8, 128), F32),
            pltpu.VMEM((RANK, D), F32),
            pltpu.VMEM((RANK, D // 2), F32),
            pltpu.VMEM((16, RANK, 128), BF16),
            pltpu.VMEM((16, RANK, 128), BF16),
            pltpu.VMEM((8, RANK, 128), BF16),
            pltpu.VMEM((2, 16, RANK, 128), BF16),
            dma((5,)), dma((4,)), dma((4,)), dma((4,)), dma((4,)), dma((4,)), dma((4,)), dma((5, 4)),
            dma((3, 4)), dma((2, 4)), dma((4, 4)),
            dma((5, GROUPS)), dma((5, GROUPS)), dma((3,)), dma((3,)), dma((5,)), dma((5,)),
        ],
        compiler_params=pltpu.CompilerParams(
            collective_id=0, has_side_effects=True, vmem_limit_bytes=60 << 20
        ),
        name="attend",
    )(lengths, queries[0], keys[0], values[0], out_grad[0], q_init)
    return (p_hat, q_new)


def solution(mesh):
    placed = (
        P("dp", "ctx", None),
        P("dp", "ctx", None),
        P("dp", "ctx", None),
        P("dp", "ctx", None),
        P(),
        P("dp"),
    )
    return jax.shard_map(local, mesh=mesh, in_specs=placed, out_specs=(P(), P()), check_vma=False)
```

```python
import functools

import jax
import jax.numpy as jnp
from jax import lax
from jax.experimental import pallas as pl
from jax.experimental.pallas import tpu as pltpu
from jax.sharding import PartitionSpec as P

HD = 128
FR = 256
HEADS = 16
WIDTH = HEADS * HD
D = 4096
RANK = 64
REACH = 8
GROUPS = 4
PER = HEADS // GROUPS
PARTS = GROUPS
CH = WIDTH // PARTS
LOG2E = 1.4426950408889634
SCALE2 = LOG2E / HD**0.5
LOW = -1e30
MESH = pl.DeviceIdType.MESH
F32 = jnp.float32
BF16 = jnp.bfloat16


def nt(a, b, **kw):
    return lax.dot_general(a, b, (((1,), (1,)), ((), ())), preferred_element_type=F32, **kw)


def nn(a, b, **kw):
    return lax.dot_general(a, b, (((1,), (0,)), ((), ())), preferred_element_type=F32, **kw)


def kernel(
    len_ref, q_any, k_any, v_any, g_any, qi_any, phat_ref, qnew_ref,
    q_ref, k_ref, v_ref, g_ref, qi_ref,
    qbuf, ebuf, mx, lg_out, lg_in, ls_out, ls_in, fac, pj_in, yacc, mp_out, mp_in,
    xp, xr, xz, psum, xq, xq_c, xq_b, xq_xy, xq_z, qg,
    ss_in, ss_x, ss_dm, ss_dp, ss_f1, ss_f3, ss_t, ss_sib, rs_slot, rs_h, rs_sib,
    ss_g, rs_g, ss_o, rs_o, ss_q, rs_q,
):
    dp = lax.axis_index("dp")
    ctx = lax.axis_index("ctx")
    zlo, y = dp // 4, dp % 4
    x, zh, core = ctx // 8, (ctx // 2) % 4, ctx % 2
    plane = x * 4 + y
    zz = zh * 2 + zlo
    rank = plane * 2 + core

    def at_ctx(i):
        return (dp, lax.rem(i + 64, 32))

    def at_plane(p):
        return (zlo * 4 + p % 4, (p // 4) * 8 + zh * 2 + core)

    def at_rank(r):
        return (zlo * 4 + (r // 2) % 4, (r // 8) * 8 + zh * 2 + r % 2)

    def at_z(z):
        return ((z % 2) * 4 + y, x * 8 + (z // 2) * 2 + core)

    sibling = (dp, ctx + 1 - 2 * core)
    up = (dp, x * 8 + ((zh + 1) % 4) * 2 + core)
    down = (dp, x * 8 + ((zh + 3) % 4) * 2 + core)
    left = at_ctx(ctx - 8)

    def rc(src, dst, ss, rs, device):
        return pltpu.make_async_remote_copy(
            src_ref=src, dst_ref=dst, send_sem=ss, recv_sem=rs, device_id=device, device_id_type=MESH
        )

    def each(lo, hi, do):
        def body(i, c):
            do(i)
            return c

        lax.fori_loop(lo, hi, body, 0)

    loads = [
        pltpu.make_async_copy(a, b, ss_in.at[i])
        for i, (a, b) in enumerate(
            ((q_any, q_ref), (k_any, k_ref), (g_any, g_ref), (qi_any, qi_ref), (v_any, v_ref))
        )
    ]
    for load in loads:
        load.start()

    bar = pltpu.get_barrier_semaphore()

    def greet(device):
        pl.semaphore_signal(bar, 1, device_id=device, device_id_type=MESH)

    def greet_ctx(i):
        greet(at_ctx(ctx + i))
        greet(at_ctx(ctx - i))

    each(1, REACH + 1, greet_ctx)
    each(1, 32, lambda i: greet(at_rank((rank + i) % 32)))
    each(1, 8, lambda i: greet(at_z((zz + i) % 8)))
    pl.semaphore_wait(bar, 2 * REACH + 31 + 7)

    def cols(g):
        return pl.ds(g * CH, CH)

    def chunk(d, g):
        return qbuf.at[d, :, cols(g)]

    mid = (zh == 1) | (zh == 2)
    edge = (zh == 0) | (zh == 3)

    def c_x(g):
        return rc(q_ref.at[:, cols(g)], chunk(8, g), ss_x.at[g], rs_slot.at[2, g], left)

    def sub(ref, p):
        return ref.at[:, pl.ds(p * CH // 2, CH // 2)]

    def c_x0(p):
        return rc(sub(q_ref, p), sub(qbuf.at[8], p), ss_x.at[4 * p], rs_slot.at[2, 4 * p], left)

    def pass_half(p):
        src = sub(qbuf.at[8], p)

        @pl.when(zh == 0)
        def _():
            rc(src, sub(qbuf.at[2], p), ss_dm.at[0], rs_slot.at[0, 0], down).start()

        @pl.when(zh < 3)
        def _():
            rc(src, sub(qbuf.at[6], p), ss_dp.at[0], rs_slot.at[1, 0], up).start()

    def c_dm(g, own):
        src = q_ref.at[:, cols(g)] if own else chunk(8, g)
        return rc(src, chunk(2, g), ss_dm.at[g], rs_slot.at[0, g], down)

    def c_dp(g, own):
        src = q_ref.at[:, cols(g)] if own else chunk(8, g)
        return rc(src, chunk(6, g), ss_dp.at[g], rs_slot.at[1, g], up)

    def c_f1(g):
        slot, sem = jnp.where(zh == 0, 0, 4), jnp.where(zh == 0, 1, 0)
        return rc(chunk(2, g), chunk(slot, g), ss_f1.at[g], rs_h.at[sem, g], down)

    def c_f3(g):
        slot, sem = jnp.where(zh == 3, 0, 4), jnp.where(zh == 3, 1, 0)
        return rc(chunk(6, g), chunk(slot, g), ss_f3.at[g], rs_h.at[sem, g], up)

    def forwards(g):
        return edge if g < PARTS // 2 else mid

    def c_t(g):
        far = (dp, lax.rem(ctx + jnp.where(zh == 0, 8, 24), 32))
        return rc(chunk(0, g), chunk(4, g), ss_t.at[g], rs_h.at[0, g], far)

    def c_sib(k, g):
        if k == 0:
            src, to = q_ref.at[:, cols(g)], 1
        elif k == 4:
            src, to = chunk(8, g), 7
        else:
            src, to = chunk(2 * k, g), 2 * k - 1 + 2 * core
        return rc(src, chunk(to, g), ss_sib.at[k, g], rs_sib.at[(to - 1) // 2, g], sibling)

    def got(dst, rs):
        rc(dst, dst, ss_x.at[0], rs, sibling).wait_recv()

    def left_all(src, ss):
        rc(src, src, ss, rs_g.at[0, 0], sibling).wait_send()

    keep_row = lax.broadcasted_iota(jnp.int32, (FR, FR), 0)
    keep_col = lax.broadcasted_iota(jnp.int32, (FR, FR), 1)

    def fold(a):
        return jnp.concatenate([a[:, : FR // 2], a[:, FR // 2 :]], axis=0)

    def unfold(a):
        return jnp.concatenate([a[:PER], a[PER:]], axis=1)

    def stat(ref, d, g):
        return ref.at[pl.ds(pl.multiple_of((d * GROUPS + g) * 8, 8), 8), :]

    def unit(d, g):
        tops, sums = [], []
        for i in range(PER):
            h = g * PER + i
            hs = slice(h * HD, h * HD + HD)
            qh = q_ref[:, hs] if isinstance(d, int) and d == 0 else qbuf[d, :, hs]
            s = nt(k_ref[:, hs], qh)
            if isinstance(d, int) and d == 0:
                s = jnp.where(keep_row <= keep_col, s, LOW)
            elif isinstance(d, int) and d == 8:
                s = jnp.where(keep_row > keep_col, s, LOW)
            m = jnp.max(s, axis=0, keepdims=True)
            e = jnp.exp2((s - m) * SCALE2)
            ebuf[d * HEADS + h] = e.astype(BF16)
            tops.append(m)
            sums.append(jnp.sum(e, axis=0, keepdims=True))
        top = jnp.concatenate(tops, axis=0) * SCALE2
        logs = top + jnp.log2(jnp.concatenate(sums, axis=0))
        stat(mx, d, g)[...] = jnp.concatenate([top, top], axis=0)
        lg_out[g, d] = fold(logs)

    def early_odd(g):
        for k in (0, 3, 1 + core):
            on_sib(g, k)
        unit(1, g)
        unit(7, g)
        unit(3 + 2 * core, g)

    def on_x(g):
        if g == 0:
            for p in range(2):
                got(sub(qbuf.at[8], p), rs_slot.at[2, 4 * p])
                pass_half(p)
        else:
            got(chunk(8, g), rs_slot.at[2, g])

        @pl.when(core == 0)
        def _():
            c_sib(4, g).start()

    def on_1(g):
        got(chunk(2, g), rs_slot.at[0, g])
        pl.when(forwards(g))(lambda: c_f1(g).start())
        c_sib(1, g).start()

    def on_3(g):
        got(chunk(6, g), rs_slot.at[1, g])
        pl.when(forwards(g))(lambda: c_f3(g).start())
        c_sib(3, g).start()

    def on_t(g):
        @pl.when(edge)
        def _():
            got(chunk(0, g), rs_h.at[1, g])
            c_t(g).start()

    def on_2(g):
        got(chunk(4, g), rs_h.at[0, g])
        c_sib(2, g).start()

    def on_sib(g, k):
        got(chunk(2 * k + 1, g), rs_sib.at[k, g])

    def c_lg(d, g):
        return rc(lg_out.at[g, d], lg_in.at[g, d], ss_g.at[0, g], rs_g.at[0, g], at_ctx(ctx + d))

    def c_ls(d, g):
        return rc(ls_out.at[g], ls_in.at[g, d], ss_g.at[1, g], rs_g.at[1, g], at_ctx(ctx - d))

    def c_p(k):
        return rc(pj_in.at[0], pj_in.at[2 * k], ss_o.at[0], rs_o.at[0], at_ctx(ctx - 2 * k))

    def c_ps(k):
        src, to = (pj_in.at[0], 1) if k == 0 else (pj_in.at[2 * k], 2 * k - 1 + 2 * core)
        if k == 4:
            to = 7
        return rc(src, pj_in.at[to], ss_o.at[2], rs_o.at[2], sibling)

    def share_proj():
        got(pj_in.at[pl.ds(1, 4)], rs_o.at[0])
        for k in (1, 2, 3):
            c_ps(k).start()

        @pl.when(core == 0)
        def _():
            c_ps(4).start()

        @pl.when(core == 1)
        def _():
            c_ps(0).start()

    def c_m(d):
        return rc(mp_out.at[d], mp_in.at[d], ss_o.at[1], rs_o.at[1], at_ctx(ctx + d))

    def stage_a(g):
        each(1, REACH + 1, lambda d: c_lg(d, g).start())

    def stage_b(g):
        got(lg_in.at[g, pl.ds(1, REACH)], rs_g.at[0, g])
        logs = [lg_out[g, 0]]
        for d in range(1, REACH + 1):
            logs.append(jnp.where(ctx >= d, lg_in[g, d], LOW))
        top = functools.reduce(jnp.maximum, logs)
        total = functools.reduce(jnp.add, [jnp.exp2(a - top) for a in logs])
        ls_out[g] = top + jnp.log2(total)
        each(1, REACH + 1, lambda d: c_ls(d, g).start())

    def c_rs(k, g):
        r = (rank + k) % 32
        return rc(xp.at[g, r], xr.at[g, rank], ss_g.at[2, g], rs_g.at[2, g], at_rank(r))

    def c_z(k, g):
        return rc(xz.at[g, zz], xz.at[g, zz], ss_g.at[3, g], rs_g.at[3, g], at_z((zz + k) % 8))

    def c_ag(k, g):
        ref = psum.at[g, rank]
        return rc(ref, ref, ss_g.at[4, g], rs_g.at[4, g], at_rank((rank + k) % 32))

    def stage_c(g):
        got(ls_in.at[g, pl.ds(1, REACH)], rs_g.at[1, g])
        lane = lax.broadcasted_iota(jnp.int32, (PER, FR), 1)
        accs = [jnp.zeros((RANK, FR), F32) for _ in range(PER)]
        for d in range(REACH + 1):
            ls = unfold(ls_out[g] if d == 0 else ls_in[g, d])
            pos = (ctx + d) * FR + lane
            f = jnp.exp2(stat(mx, d, g)[...][:PER] - ls)
            f = jnp.where((pos < len_ref[0]) & (ctx + d < 32), f, 0.0)
            stat(fac, d, g)[...] = jnp.concatenate([f, f], axis=0)
            pj = pj_in[d].astype(F32)
            for i in range(PER):
                pf = (pj * f[i : i + 1, :]).astype(BF16)
                accs[i] = accs[i] + nt(pf, ebuf[d * HEADS + g * PER + i])
        for i in range(PER):
            hs = slice((g * PER + i) * HD, (g * PER + i + 1) * HD)
            xp[g, 8 * i : 8 * i + 8] = nn(accs[i].astype(BF16), v_ref[:, hs]).reshape(8, 8, HD)
        each(1, 32, lambda k: c_rs(k, g).start())

    def stage_f(g):
        xr[g, rank] = xp[g, rank]
        got(xr.at[g, pl.ds(0, 31)], rs_g.at[2, g])
        total = xr[g, 0]
        for r in range(1, 32):
            total = total + xr[g, r]
        xz[g, zz] = total
        each(1, 8, lambda k: c_z(k, g).start())

    def stage_g(g):
        got(xz.at[g, pl.ds(0, 7)], rs_g.at[3, g])
        total = xz[g, 0]
        for z in range(1, 8):
            total = total + xz[g, z]
        psum[g, rank] = total
        each(1, 32, lambda k: c_ag(k, g).start())

    def p_head(g, i):
        return psum[g, 8 * i : 8 * i + 8].reshape(RANK, HD)

    def stage_i(g):
        got(psum.at[g, pl.ds(0, 31)], rs_g.at[4, g])
        us = []
        for i in range(PER):
            hs = slice((g * PER + i) * HD, (g * PER + i + 1) * HD)
            us.append(nt(p_head(g, i).astype(BF16), v_ref[:, hs]).astype(BF16))

        def part_of(d, start):
            f = stat(fac, d, g)[...]
            acc = start
            for i in range(PER):
                acc = acc + nn(us[i], ebuf[d * HEADS + g * PER + i]) * f[i : i + 1, :]
            return acc

        for i in range(REACH + 1):
            d = REACH - i
            acc = part_of(d, jnp.zeros((RANK, FR), F32) if g == 0 else yacc[d])
            if g < GROUPS - 1 or d == 0:
                yacc[d] = acc
            else:
                mp_out[d] = acc.astype(BF16)
                c_m(d).start()

    loads[0].wait()
    for g in range(PARTS):
        if g == 0:
            c_x0(0).start()
            c_x0(1).start()
        else:
            c_x(g).start()

        @pl.when(core == 1)
        def _():
            c_sib(0, g).start()

    early = PARTS // 2

    def own_down(g):
        pl.when(zh > 0)(lambda: c_dm(g, True).start())

    def own_up(g):
        pl.when(zh == 3)(lambda: c_dp(g, True).start())

    for g in range(PARTS):
        own_down(g)
        if g < early:
            own_up(g)

    def pass_on(g):
        if g < early:
            pl.when(zh == 0)(lambda: c_dm(g, False).start())
        pl.when(zh < 3)(lambda: c_dp(g, False).start())

    def late_down():
        for g in range(early, PARTS):
            pl.when(zh == 0)(lambda: c_dm(g, False).start())

    def late_up():
        for g in range(early, PARTS):
            own_up(g)

    for load in loads[1:4]:
        load.wait()
    pj_in[0] = nt(qi_ref[...], g_ref[...]).astype(BF16)
    each(1, 5, lambda k: c_p(k).start())
    loads[4].wait()
    on_x(0)
    unit(0, 0)
    unit(8, 0)
    on_x(1)
    pass_on(1)
    unit(0, 1)
    unit(8, 1)
    on_1(0)
    on_x(2)
    pass_on(2)
    on_3(0)
    on_x(3)
    pass_on(3)
    on_1(1)
    late_down()
    on_3(1)
    late_up()
    unit(0, 2)
    unit(8, 2)
    unit(0, 3)
    unit(8, 3)
    unit(2, 0)
    unit(6, 0)
    early_odd(0)
    unit(2, 1)
    unit(6, 1)
    on_t(0)
    early_odd(1)
    on_1(2)
    on_3(2)
    unit(2, 2)
    unit(6, 2)
    on_t(1)
    early_odd(2)
    on_1(3)
    on_3(3)
    unit(2, 3)
    unit(6, 3)
    early_odd(3)

    def complete(g):
        on_2(g)
        unit(4, g)
        on_sib(g, 2 - core)
        unit(5 - 2 * core, g)
        stage_a(g)

    complete(0)
    share_proj()
    complete(2)
    complete(1)
    got(pj_in.at[pl.ds(1, 4)], rs_o.at[2])
    stage_b(0)
    complete(3)
    stage_b(2)
    stage_b(1)
    stage_c(0)
    stage_b(3)
    stage_c(2)
    stage_c(1)
    stage_c(3)
    stage_f(0)
    stage_f(2)
    stage_f(1)
    stage_f(3)
    stage_g(0)
    stage_g(2)
    stage_g(1)
    stage_g(3)
    stage_i(0)
    stage_i(1)
    stage_i(2)
    stage_i(3)

    p_sum = jnp.concatenate([p_head(g, i) for g in range(GROUPS) for i in range(PER)], axis=1)
    gram = nt(p_sum, p_sum, precision=lax.Precision.HIGHEST)
    row_i = lax.broadcasted_iota(jnp.int32, (RANK, 2 * RANK), 0)
    col_i = lax.broadcasted_iota(jnp.int32, (RANK, 2 * RANK), 1)
    a = jnp.concatenate([gram, jnp.zeros((RANK, RANK), F32)], axis=1)
    a = jnp.where(col_i == row_i + RANK, 1.0, a)
    pivots = jnp.zeros((RANK, 2 * RANK), F32)
    for k in range(RANK):
        wide = jnp.broadcast_to(a[:, k : k + 1], (RANK, 2 * RANK))
        piv = wide[k : k + 1, :]
        line = a[k : k + 1, :] / piv
        pivots = jnp.where(row_i == k, piv, pivots)
        a = a - jnp.where(row_i > k, wide, 0.0) * line
    inv_low = a[:, RANK:] * (lax.rsqrt(pivots[:, RANK:]) * (WIDTH**0.5))

    got(mp_in.at[pl.ds(1, REACH)], rs_o.at[1])
    acc = yacc[0]
    for d in range(1, REACH + 1):
        acc = acc + jnp.where(ctx >= d, mp_in[d].astype(F32), 0.0)
    mapped = nn(inv_low, acc, precision=lax.Precision.HIGHEST).astype(BF16)

    half_w = D // 2
    mine = pl.ds(pl.multiple_of(core * half_w, half_w), half_w)
    other = pl.ds(pl.multiple_of((1 - core) * half_w, half_w), half_w)
    step = 512

    def q_cols(base, i):
        s = pl.ds(pl.multiple_of(base + i * step, step), step)
        xq[:, s] = nn(mapped, g_ref[:, s])

    each(0, half_w // step, lambda i: q_cols((1 - core) * half_w, i))
    cc = rc(xq.at[:, other], xq_c, ss_q.at[0], rs_q.at[0], sibling)
    cc.start()
    each(0, half_w // step, lambda i: q_cols(core * half_w, i))
    cc.wait_recv()

    def join(i):
        s = pl.ds(pl.multiple_of(i * 128, 128), 128)
        t = pl.ds(pl.multiple_of(core * half_w + i * 128, 128), 128)
        xq_b[i] = (xq_c[:, s] + xq[:, t]).astype(BF16)

    each(0, 16, join)

    def c_qx(k):
        p = (plane + k) % 16
        return rc(xq_b.at[p], xq_xy.at[plane], ss_q.at[1], rs_q.at[1], at_plane(p))

    each(1, 16, lambda k: c_qx(k).start())
    xq_xy[plane] = xq_b[plane]
    got(xq_xy.at[pl.ds(0, 15)], rs_q.at[1])
    total = xq_xy[0].astype(F32)
    for p in range(1, 16):
        total = total + xq_xy[p].astype(F32)
    xq_z[zz] = total.astype(BF16)

    def c_qz(k):
        return rc(xq_z.at[zz], xq_z.at[zz], ss_q.at[2], rs_q.at[2], at_z((zz + k) % 8))

    each(1, 8, lambda k: c_qz(k).start())
    phat_ref[...] = nn(inv_low, p_sum, precision=lax.Precision.HIGHEST)
    got(xq_z.at[pl.ds(0, 7)], rs_q.at[2])
    total = xq_z[0].astype(F32)
    for z in range(1, 8):
        total = total + xq_z[z].astype(F32)
    done = total * (1.0 / 256.0)
    qg[core, plane] = done.astype(BF16)

    def c_qa(k):
        ref = qg.at[core, plane]
        return rc(ref, ref, ss_q.at[3], rs_q.at[3], at_plane((plane + k) % 16))

    each(1, 16, lambda k: c_qa(k).start())
    got(qg.at[core, pl.ds(0, 15)], rs_q.at[3])
    c2 = rc(qg.at[core], qg.at[core], ss_q.at[4], rs_q.at[4], sibling)
    c2.start()
    got(qg.at[1 - core], rs_q.at[4])
    for i in range(32):
        qnew_ref[:, i * 128 : i * 128 + 128] = qg[i // 16, i % 16].astype(F32)

    for g in range(PARTS):
        if g == 0:
            c_x0(0).wait_send()
            c_x0(1).wait_send()
        else:
            c_x(g).wait_send()
        c_dm(g, True).wait_send()
        c_dp(g, True).wait_send()

        @pl.when(forwards(g))
        def _():
            c_f1(g).wait_send()
            c_f3(g).wait_send()

        for k in (1, 2, 3):
            c_sib(k, g).wait_send()

        if g < PARTS // 2:

            @pl.when(edge)
            def _():
                c_t(g).wait_send()

        @pl.when(core == 1)
        def _():
            c_sib(0, g).wait_send()

        @pl.when(core == 0)
        def _():
            c_sib(4, g).wait_send()

    for g in range(GROUPS):
        left_all(lg_in.at[g, pl.ds(0, REACH)], ss_g.at[0, g])
        left_all(ls_in.at[g, pl.ds(0, REACH)], ss_g.at[1, g])
        left_all(xr.at[g, pl.ds(0, 31)], ss_g.at[2, g])
        left_all(xz.at[g, pl.ds(0, 7)], ss_g.at[3, g])
        left_all(psum.at[g, pl.ds(0, 31)], ss_g.at[4, g])
    left_all(pj_in.at[pl.ds(0, 4)], ss_o.at[0])
    left_all(pj_in.at[pl.ds(0, 4)], ss_o.at[2])
    left_all(mp_in.at[pl.ds(0, REACH)], ss_o.at[1])
    cc.wait_send()
    left_all(xq_xy.at[pl.ds(0, 15)], ss_q.at[1])
    left_all(xq_z.at[pl.ds(0, 7)], ss_q.at[2])
    left_all(qg.at[core, pl.ds(0, 15)], ss_q.at[3])
    c2.wait_send()


def hand_over(p_in, q_in, p_out, q_out):
    p_out[...] = p_in[...]
    q_out[...] = q_in[...]


def local(queries, keys, values, out_grad, q_init, lengths):
    dma = pltpu.SemaphoreType.DMA
    n = REACH + 1
    vm = pl.BlockSpec(memory_space=pltpu.VMEM)
    outs = pl.pallas_call(
        kernel,
        out_shape=(
            jax.ShapeDtypeStruct((RANK, WIDTH), F32),
            jax.ShapeDtypeStruct((RANK, D), F32),
        ),
        in_specs=[pl.BlockSpec(memory_space=pltpu.SMEM)] + [pl.BlockSpec(memory_space=pl.ANY)] * 5,
        out_specs=(vm, vm),
        scratch_shapes=[
            pltpu.VMEM((FR, WIDTH), BF16),
            pltpu.VMEM((FR, WIDTH), BF16),
            pltpu.VMEM((FR, WIDTH), BF16),
            pltpu.VMEM((FR, D), BF16),
            pltpu.VMEM((RANK, D), BF16),
            pltpu.VMEM((n, FR, WIDTH), BF16),
            pltpu.VMEM((n * HEADS, FR, FR), BF16),
            pltpu.VMEM((n * GROUPS * 8, FR), F32),
            pltpu.VMEM((GROUPS, n, 8, 128), F32),
            pltpu.VMEM((GROUPS, n, 8, 128), F32),
            pltpu.VMEM((GROUPS, 8, 128), F32),
            pltpu.VMEM((GROUPS, n, 8, 128), F32),
            pltpu.VMEM((n * GROUPS * 8, FR), F32),
            pltpu.VMEM((n, RANK, FR), BF16),
            pltpu.VMEM((n, RANK, FR), F32),
            pltpu.VMEM((n, RANK, FR), BF16),
            pltpu.VMEM((n, RANK, FR), BF16),
            pltpu.VMEM((GROUPS, 32, 8, 128), F32),
            pltpu.VMEM((GROUPS, 32, 8, 128), F32),
            pltpu.VMEM((GROUPS, 8, 8, 128), F32),
            pltpu.VMEM((GROUPS, 32, 8, 128), F32),
            pltpu.VMEM((RANK, D), F32),
            pltpu.VMEM((RANK, D // 2), F32),
            pltpu.VMEM((16, RANK, 128), BF16),
            pltpu.VMEM((16, RANK, 128), BF16),
            pltpu.VMEM((8, RANK, 128), BF16),
            pltpu.VMEM((2, 16, RANK, 128), BF16),
            dma((5,)), dma((5,)), dma((4,)), dma((4,)), dma((4,)), dma((4,)), dma((4,)), dma((5, 4)),
            dma((3, 5)), dma((2, 4)), dma((4, 4)),
            dma((5, GROUPS)), dma((5, GROUPS)), dma((3,)), dma((3,)), dma((5,)), dma((5,)),
        ],
        compiler_params=pltpu.CompilerParams(
            collective_id=0, has_side_effects=True, vmem_limit_bytes=60 << 20
        ),
        name="attend",
    )(lengths, queries[0], keys[0], values[0], out_grad[0], q_init)
    return pl.pallas_call(
        hand_over,
        out_shape=tuple(jax.ShapeDtypeStruct(o.shape, F32) for o in outs),
        in_specs=[vm] * 2,
        out_specs=(vm,) * 2,
        name="hand_over",
    )(*outs)


def solution(mesh):
    placed = (
        P("dp", "ctx", None),
        P("dp", "ctx", None),
        P("dp", "ctx", None),
        P("dp", "ctx", None),
        P(),
        P("dp"),
    )
    return jax.shard_map(local, mesh=mesh, in_specs=placed, out_specs=(P(), P()), check_vma=False)
```

```python
import functools

import jax
import jax.numpy as jnp
from jax import lax
from jax.experimental import pallas as pl
from jax.experimental.pallas import tpu as pltpu
from jax.sharding import PartitionSpec as P

HD = 128
FR = 256
HEADS = 16
WIDTH = HEADS * HD
D = 4096
RANK = 64
REACH = 8
GROUPS = 4
PER = HEADS // GROUPS
PARTS = GROUPS
CH = WIDTH // PARTS
LOG2E = 1.4426950408889634
SCALE2 = LOG2E / HD**0.5
LOW = -1e30
MESH = pl.DeviceIdType.MESH
F32 = jnp.float32
BF16 = jnp.bfloat16


def nt(a, b, **kw):
    return lax.dot_general(a, b, (((1,), (1,)), ((), ())), preferred_element_type=F32, **kw)


def nn(a, b, **kw):
    return lax.dot_general(a, b, (((1,), (0,)), ((), ())), preferred_element_type=F32, **kw)


def kernel(
    len_ref, q_any, k_any, v_any, g_any, qi_any, phat_ref, qnew_ref,
    q_ref, k_ref, v_ref, g_ref, qi_ref,
    qbuf, ebuf, mx, lg_out, lg_in, ls_out, ls_in, fac, pj_in, yacc, mp_out, mp_in,
    xp, xr, xz, psum, xq, xq_c, xq_b, xq_xy, xq_z, qg,
    ss_in, ss_x, ss_dm, ss_dp, ss_f1, ss_f3, ss_t, ss_sib, rs_slot, rs_h, rs_sib,
    ss_g, rs_g, ss_o, rs_o, ss_q, rs_q,
):
    dp = lax.axis_index("dp")
    ctx = lax.axis_index("ctx")
    zlo, y = dp // 4, dp % 4
    x, zh, core = ctx // 8, (ctx // 2) % 4, ctx % 2
    plane = x * 4 + y
    zz = zh * 2 + zlo
    rank = plane * 2 + core

    def at_ctx(i):
        return (dp, lax.rem(i + 64, 32))

    def at_plane(p):
        return (zlo * 4 + p % 4, (p // 4) * 8 + zh * 2 + core)

    def at_rank(r):
        return (zlo * 4 + (r // 2) % 4, (r // 8) * 8 + zh * 2 + r % 2)

    def at_z(z):
        return ((z % 2) * 4 + y, x * 8 + (z // 2) * 2 + core)

    sibling = (dp, ctx + 1 - 2 * core)
    up = (dp, x * 8 + ((zh + 1) % 4) * 2 + core)
    down = (dp, x * 8 + ((zh + 3) % 4) * 2 + core)
    left = at_ctx(ctx - 8)

    def rc(src, dst, ss, rs, device):
        return pltpu.make_async_remote_copy(
            src_ref=src, dst_ref=dst, send_sem=ss, recv_sem=rs, device_id=device, device_id_type=MESH
        )

    def each(lo, hi, do):
        def body(i, c):
            do(i)
            return c

        lax.fori_loop(lo, hi, body, 0)

    loads = [
        pltpu.make_async_copy(a, b, ss_in.at[i])
        for i, (a, b) in enumerate(
            ((q_any, q_ref), (k_any, k_ref), (g_any, g_ref), (qi_any, qi_ref), (v_any, v_ref))
        )
    ]
    for load in loads:
        load.start()

    bar = pltpu.get_barrier_semaphore()

    def greet(device):
        pl.semaphore_signal(bar, 1, device_id=device, device_id_type=MESH)

    def greet_ctx(i):
        greet(at_ctx(ctx + i))
        greet(at_ctx(ctx - i))

    each(1, REACH + 1, greet_ctx)
    each(1, 32, lambda i: greet(at_rank((rank + i) % 32)))
    each(1, 8, lambda i: greet(at_z((zz + i) % 8)))
    pl.semaphore_wait(bar, 2 * REACH + 31 + 7)

    def cols(g):
        return pl.ds(g * CH, CH)

    def chunk(d, g):
        return qbuf.at[d, :, cols(g)]

    mid = (zh == 1) | (zh == 2)
    edge = (zh == 0) | (zh == 3)

    def c_x(g):
        return rc(q_ref.at[:, cols(g)], chunk(8, g), ss_x.at[g], rs_slot.at[2, g], left)

    def sub(ref, p):
        return ref.at[:, pl.ds(p * CH // 4, CH // 4)]

    def c_x0(p):
        i = 0 if p == 0 else 3 + p
        return rc(sub(q_ref, p), sub(qbuf.at[8], p), ss_x.at[i], rs_slot.at[2, i], left)

    def pass_piece(p):
        src = sub(qbuf.at[8], p)

        @pl.when(zh == 0)
        def _():
            rc(src, sub(qbuf.at[2], p), ss_dm.at[0], rs_slot.at[0, 0], down).start()

        @pl.when(zh < 3)
        def _():
            rc(src, sub(qbuf.at[6], p), ss_dp.at[0], rs_slot.at[1, 0], up).start()

    def c_dm(g, own):
        src = q_ref.at[:, cols(g)] if own else chunk(8, g)
        return rc(src, chunk(2, g), ss_dm.at[g], rs_slot.at[0, g], down)

    def c_dp(g, own):
        src = q_ref.at[:, cols(g)] if own else chunk(8, g)
        return rc(src, chunk(6, g), ss_dp.at[g], rs_slot.at[1, g], up)

    def c_f1(g):
        slot, sem = jnp.where(zh == 0, 0, 4), jnp.where(zh == 0, 1, 0)
        return rc(chunk(2, g), chunk(slot, g), ss_f1.at[g], rs_h.at[sem, g], down)

    def c_f3(g):
        slot, sem = jnp.where(zh == 3, 0, 4), jnp.where(zh == 3, 1, 0)
        return rc(chunk(6, g), chunk(slot, g), ss_f3.at[g], rs_h.at[sem, g], up)

    def forwards(g):
        return edge if g < PARTS // 2 else mid

    def c_t(g):
        far = (dp, lax.rem(ctx + jnp.where(zh == 0, 8, 24), 32))
        return rc(chunk(0, g), chunk(4, g), ss_t.at[g], rs_h.at[0, g], far)

    def c_sib(k, g):
        if k == 0:
            src, to = q_ref.at[:, cols(g)], 1
        elif k == 4:
            src, to = chunk(8, g), 7
        else:
            src, to = chunk(2 * k, g), 2 * k - 1 + 2 * core
        return rc(src, chunk(to, g), ss_sib.at[k, g], rs_sib.at[(to - 1) // 2, g], sibling)

    def got(dst, rs):
        rc(dst, dst, ss_x.at[0], rs, sibling).wait_recv()

    def left_all(src, ss):
        rc(src, src, ss, rs_g.at[0, 0], sibling).wait_send()

    keep_row = lax.broadcasted_iota(jnp.int32, (FR, FR), 0)
    keep_col = lax.broadcasted_iota(jnp.int32, (FR, FR), 1)

    def fold(a):
        return jnp.concatenate([a[:, : FR // 2], a[:, FR // 2 :]], axis=0)

    def unfold(a):
        return jnp.concatenate([a[:PER], a[PER:]], axis=1)

    def stat(ref, d, g):
        return ref.at[pl.ds(pl.multiple_of((d * GROUPS + g) * 8, 8), 8), :]

    def unit(d, g):
        tops, sums = [], []
        for i in range(PER):
            h = g * PER + i
            hs = slice(h * HD, h * HD + HD)
            qh = q_ref[:, hs] if isinstance(d, int) and d == 0 else qbuf[d, :, hs]
            s = nt(k_ref[:, hs], qh)
            if isinstance(d, int) and d == 0:
                s = jnp.where(keep_row <= keep_col, s, LOW)
            elif isinstance(d, int) and d == 8:
                s = jnp.where(keep_row > keep_col, s, LOW)
            m = jnp.max(s, axis=0, keepdims=True)
            e = jnp.exp2((s - m) * SCALE2)
            ebuf[d * HEADS + h] = e.astype(BF16)
            tops.append(m)
            sums.append(jnp.sum(e, axis=0, keepdims=True))
        top = jnp.concatenate(tops, axis=0) * SCALE2
        logs = top + jnp.log2(jnp.concatenate(sums, axis=0))
        stat(mx, d, g)[...] = jnp.concatenate([top, top], axis=0)
        lg_out[g, d] = fold(logs)

    def early_odd(g):
        for k in (0, 3, 1 + core):
            on_sib(g, k)
        unit(1, g)
        unit(7, g)
        unit(3 + 2 * core, g)

    def on_x(g):
        if g == 0:
            for p in range(4):
                got(sub(qbuf.at[8], p), rs_slot.at[2, 0 if p == 0 else 3 + p])
                pass_piece(p)
        else:
            got(chunk(8, g), rs_slot.at[2, g])

        @pl.when(core == 0)
        def _():
            c_sib(4, g).start()

    def on_1(g):
        got(chunk(2, g), rs_slot.at[0, g])
        pl.when(forwards(g))(lambda: c_f1(g).start())
        c_sib(1, g).start()

    def on_3(g):
        got(chunk(6, g), rs_slot.at[1, g])
        pl.when(forwards(g))(lambda: c_f3(g).start())
        c_sib(3, g).start()

    def on_t(g):
        @pl.when(edge)
        def _():
            got(chunk(0, g), rs_h.at[1, g])
            c_t(g).start()

    def on_2(g):
        got(chunk(4, g), rs_h.at[0, g])
        c_sib(2, g).start()

    def on_sib(g, k):
        got(chunk(2 * k + 1, g), rs_sib.at[k, g])

    def c_lg(d, g):
        return rc(lg_out.at[g, d], lg_in.at[g, d], ss_g.at[0, g], rs_g.at[0, g], at_ctx(ctx + d))

    def c_ls(d, g):
        return rc(ls_out.at[g], ls_in.at[g, d], ss_g.at[1, g], rs_g.at[1, g], at_ctx(ctx - d))

    def c_p(k):
        return rc(pj_in.at[0], pj_in.at[2 * k], ss_o.at[0], rs_o.at[0], at_ctx(ctx - 2 * k))

    def c_ps(k):
        src, to = (pj_in.at[0], 1) if k == 0 else (pj_in.at[2 * k], 2 * k - 1 + 2 * core)
        if k == 4:
            to = 7
        return rc(src, pj_in.at[to], ss_o.at[2], rs_o.at[2], sibling)

    def share_proj():
        got(pj_in.at[pl.ds(1, 4)], rs_o.at[0])
        for k in (1, 2, 3):
            c_ps(k).start()

        @pl.when(core == 0)
        def _():
            c_ps(4).start()

        @pl.when(core == 1)
        def _():
            c_ps(0).start()

    def c_m(d):
        return rc(mp_out.at[d], mp_in.at[d], ss_o.at[1], rs_o.at[1], at_ctx(ctx + d))

    def stage_a(g):
        each(1, REACH + 1, lambda d: c_lg(d, g).start())

    def stage_b(g):
        got(lg_in.at[g, pl.ds(1, REACH)], rs_g.at[0, g])
        logs = [lg_out[g, 0]]
        for d in range(1, REACH + 1):
            logs.append(jnp.where(ctx >= d, lg_in[g, d], LOW))
        top = functools.reduce(jnp.maximum, logs)
        total = functools.reduce(jnp.add, [jnp.exp2(a - top) for a in logs])
        ls_out[g] = top + jnp.log2(total)
        each(1, REACH + 1, lambda d: c_ls(d, g).start())

    def c_rs(k, g):
        r = (rank + k) % 32
        return rc(xp.at[g, r], xr.at[g, rank], ss_g.at[2, g], rs_g.at[2, g], at_rank(r))

    def c_z(k, g):
        return rc(xz.at[g, zz], xz.at[g, zz], ss_g.at[3, g], rs_g.at[3, g], at_z((zz + k) % 8))

    def c_ag(k, g):
        ref = psum.at[g, rank]
        return rc(ref, ref, ss_g.at[4, g], rs_g.at[4, g], at_rank((rank + k) % 32))

    def stage_c(g):
        got(ls_in.at[g, pl.ds(1, REACH)], rs_g.at[1, g])
        lane = lax.broadcasted_iota(jnp.int32, (PER, FR), 1)
        accs = [jnp.zeros((RANK, FR), F32) for _ in range(PER)]
        for d in range(REACH + 1):
            ls = unfold(ls_out[g] if d == 0 else ls_in[g, d])
            pos = (ctx + d) * FR + lane
            f = jnp.exp2(stat(mx, d, g)[...][:PER] - ls)
            f = jnp.where((pos < len_ref[0]) & (ctx + d < 32), f, 0.0)
            stat(fac, d, g)[...] = jnp.concatenate([f, f], axis=0)
            pj = pj_in[d].astype(F32)
            for i in range(PER):
                pf = (pj * f[i : i + 1, :]).astype(BF16)
                accs[i] = accs[i] + nt(pf, ebuf[d * HEADS + g * PER + i])
        for i in range(PER):
            hs = slice((g * PER + i) * HD, (g * PER + i + 1) * HD)
            xp[g, 8 * i : 8 * i + 8] = nn(accs[i].astype(BF16), v_ref[:, hs]).reshape(8, 8, HD)
        each(1, 32, lambda k: c_rs(k, g).start())

    def stage_f(g):
        xr[g, rank] = xp[g, rank]
        got(xr.at[g, pl.ds(0, 31)], rs_g.at[2, g])
        total = xr[g, 0]
        for r in range(1, 32):
            total = total + xr[g, r]
        xz[g, zz] = total
        each(1, 8, lambda k: c_z(k, g).start())

    def stage_g(g):
        got(xz.at[g, pl.ds(0, 7)], rs_g.at[3, g])
        total = xz[g, 0]
        for z in range(1, 8):
            total = total + xz[g, z]
        psum[g, rank] = total
        each(1, 32, lambda k: c_ag(k, g).start())

    def p_head(g, i):
        return psum[g, 8 * i : 8 * i + 8].reshape(RANK, HD)

    def stage_i(g):
        got(psum.at[g, pl.ds(0, 31)], rs_g.at[4, g])
        us = []
        for i in range(PER):
            hs = slice((g * PER + i) * HD, (g * PER + i + 1) * HD)
            us.append(nt(p_head(g, i).astype(BF16), v_ref[:, hs]).astype(BF16))

        def part_of(d, start):
            f = stat(fac, d, g)[...]
            acc = start
            for i in range(PER):
                acc = acc + nn(us[i], ebuf[d * HEADS + g * PER + i]) * f[i : i + 1, :]
            return acc

        for i in range(REACH + 1):
            d = REACH - i
            acc = part_of(d, jnp.zeros((RANK, FR), F32) if g == 0 else yacc[d])
            if g < GROUPS - 1 or d == 0:
                yacc[d] = acc
            else:
                mp_out[d] = acc.astype(BF16)
                c_m(d).start()

    loads[0].wait()
    for g in range(PARTS):
        if g == 0:
            for p in range(4):
                c_x0(p).start()
        else:
            c_x(g).start()

        @pl.when(core == 1)
        def _():
            c_sib(0, g).start()

    early = PARTS // 2

    def own_down(g):
        pl.when(zh > 0)(lambda: c_dm(g, True).start())

    def own_up(g):
        pl.when(zh == 3)(lambda: c_dp(g, True).start())

    for g in range(PARTS):
        own_down(g)
        if g < early:
            own_up(g)

    def pass_on(g):
        if g < early:
            pl.when(zh == 0)(lambda: c_dm(g, False).start())
        pl.when(zh < 3)(lambda: c_dp(g, False).start())

    def late_down():
        for g in range(early, PARTS):
            pl.when(zh == 0)(lambda: c_dm(g, False).start())

    def late_up():
        for g in range(early, PARTS):
            own_up(g)

    for load in loads[1:4]:
        load.wait()
    pj_in[0] = nt(qi_ref[...], g_ref[...]).astype(BF16)
    each(1, 5, lambda k: c_p(k).start())
    loads[4].wait()
    on_x(0)
    on_x(1)
    pass_on(1)
    unit(0, 0)
    unit(8, 0)
    on_1(0)
    on_x(2)
    pass_on(2)
    on_3(0)
    unit(0, 1)
    unit(8, 1)
    on_x(3)
    pass_on(3)
    on_1(1)
    late_down()
    on_3(1)
    late_up()
    unit(0, 2)
    unit(8, 2)
    unit(0, 3)
    unit(8, 3)
    unit(2, 0)
    unit(6, 0)
    early_odd(0)
    on_t(0)
    unit(2, 1)
    unit(6, 1)
    early_odd(1)
    on_1(2)
    on_3(2)
    on_t(1)
    unit(2, 2)
    unit(6, 2)
    early_odd(2)
    on_1(3)
    on_3(3)
    unit(2, 3)
    unit(6, 3)
    early_odd(3)

    def complete(g):
        on_2(g)
        unit(4, g)
        on_sib(g, 2 - core)
        unit(5 - 2 * core, g)
        stage_a(g)

    complete(0)
    share_proj()
    complete(2)
    complete(1)
    got(pj_in.at[pl.ds(1, 4)], rs_o.at[2])
    stage_b(0)
    complete(3)
    stage_b(2)
    stage_b(1)
    stage_c(0)
    stage_b(3)
    stage_c(2)
    stage_c(1)
    stage_c(3)
    stage_f(0)
    stage_f(2)
    stage_f(1)
    stage_f(3)
    stage_g(0)
    stage_g(2)
    stage_g(1)
    stage_g(3)
    stage_i(0)
    stage_i(1)
    stage_i(2)
    stage_i(3)

    p_sum = jnp.concatenate([p_head(g, i) for g in range(GROUPS) for i in range(PER)], axis=1)
    gram = nt(p_sum, p_sum, precision=lax.Precision.HIGHEST)
    row_i = lax.broadcasted_iota(jnp.int32, (RANK, 2 * RANK), 0)
    col_i = lax.broadcasted_iota(jnp.int32, (RANK, 2 * RANK), 1)
    a = jnp.concatenate([gram, jnp.zeros((RANK, RANK), F32)], axis=1)
    a = jnp.where(col_i == row_i + RANK, 1.0, a)
    pivots = jnp.zeros((RANK, 2 * RANK), F32)
    for k in range(RANK):
        wide = jnp.broadcast_to(a[:, k : k + 1], (RANK, 2 * RANK))
        piv = wide[k : k + 1, :]
        line = a[k : k + 1, :] / piv
        pivots = jnp.where(row_i == k, piv, pivots)
        a = a - jnp.where(row_i > k, wide, 0.0) * line
    inv_low = a[:, RANK:] * (lax.rsqrt(pivots[:, RANK:]) * (WIDTH**0.5))

    got(mp_in.at[pl.ds(1, REACH)], rs_o.at[1])
    acc = yacc[0]
    for d in range(1, REACH + 1):
        acc = acc + jnp.where(ctx >= d, mp_in[d].astype(F32), 0.0)
    mapped = nn(inv_low, acc, precision=lax.Precision.HIGHEST).astype(BF16)

    half_w = D // 2
    mine = pl.ds(pl.multiple_of(core * half_w, half_w), half_w)
    other = pl.ds(pl.multiple_of((1 - core) * half_w, half_w), half_w)
    step = 512

    def q_cols(base, i):
        s = pl.ds(pl.multiple_of(base + i * step, step), step)
        xq[:, s] = nn(mapped, g_ref[:, s])

    each(0, half_w // step, lambda i: q_cols((1 - core) * half_w, i))
    cc = rc(xq.at[:, other], xq_c, ss_q.at[0], rs_q.at[0], sibling)
    cc.start()
    each(0, half_w // step, lambda i: q_cols(core * half_w, i))
    cc.wait_recv()

    def join(i):
        s = pl.ds(pl.multiple_of(i * 128, 128), 128)
        t = pl.ds(pl.multiple_of(core * half_w + i * 128, 128), 128)
        xq_b[i] = (xq_c[:, s] + xq[:, t]).astype(BF16)

    def c_qx(k):
        p = (plane + k) % 16
        return rc(xq_b.at[p], xq_xy.at[plane], ss_q.at[1], rs_q.at[1], at_plane(p))

    def join_send(k):
        join((plane + k) % 16)
        c_qx(k).start()

    each(1, 16, join_send)
    join(plane)
    xq_xy[plane] = xq_b[plane]
    got(xq_xy.at[pl.ds(0, 15)], rs_q.at[1])
    total = xq_xy[0].astype(F32)
    for p in range(1, 16):
        total = total + xq_xy[p].astype(F32)
    xq_z[zz] = total.astype(BF16)

    def c_qz(k):
        return rc(xq_z.at[zz], xq_z.at[zz], ss_q.at[2], rs_q.at[2], at_z((zz + k) % 8))

    each(1, 8, lambda k: c_qz(k).start())
    phat_ref[...] = nn(inv_low, p_sum, precision=lax.Precision.HIGHEST)
    got(xq_z.at[pl.ds(0, 7)], rs_q.at[2])
    total = xq_z[0].astype(F32)
    for z in range(1, 8):
        total = total + xq_z[z].astype(F32)
    done = total * (1.0 / 256.0)
    qg[core, plane] = done.astype(BF16)

    def c_qa(k):
        ref = qg.at[core, plane]
        return rc(ref, ref, ss_q.at[3], rs_q.at[3], at_plane((plane + k) % 16))

    each(1, 16, lambda k: c_qa(k).start())
    got(qg.at[core, pl.ds(0, 15)], rs_q.at[3])
    c2 = rc(qg.at[core], qg.at[core], ss_q.at[4], rs_q.at[4], sibling)
    c2.start()
    for j in (core, 1 - core):
        if j is not core:
            got(qg.at[j], rs_q.at[4])
        for i in range(16):
            s = pl.ds(pl.multiple_of(j * half_w + i * 128, 128), 128)
            qnew_ref[:, s] = qg[j, i].astype(F32)

    for g in range(PARTS):
        if g == 0:
            for p in range(4):
                c_x0(p).wait_send()
        else:
            c_x(g).wait_send()
        c_dm(g, True).wait_send()
        c_dp(g, True).wait_send()

        @pl.when(forwards(g))
        def _():
            c_f1(g).wait_send()
            c_f3(g).wait_send()

        for k in (1, 2, 3):
            c_sib(k, g).wait_send()

        if g < PARTS // 2:

            @pl.when(edge)
            def _():
                c_t(g).wait_send()

        @pl.when(core == 1)
        def _():
            c_sib(0, g).wait_send()

        @pl.when(core == 0)
        def _():
            c_sib(4, g).wait_send()

    for g in range(GROUPS):
        left_all(lg_in.at[g, pl.ds(0, REACH)], ss_g.at[0, g])
        left_all(ls_in.at[g, pl.ds(0, REACH)], ss_g.at[1, g])
        left_all(xr.at[g, pl.ds(0, 31)], ss_g.at[2, g])
        left_all(xz.at[g, pl.ds(0, 7)], ss_g.at[3, g])
        left_all(psum.at[g, pl.ds(0, 31)], ss_g.at[4, g])
    left_all(pj_in.at[pl.ds(0, 4)], ss_o.at[0])
    left_all(pj_in.at[pl.ds(0, 4)], ss_o.at[2])
    left_all(mp_in.at[pl.ds(0, REACH)], ss_o.at[1])
    cc.wait_send()
    left_all(xq_xy.at[pl.ds(0, 15)], ss_q.at[1])
    left_all(xq_z.at[pl.ds(0, 7)], ss_q.at[2])
    left_all(qg.at[core, pl.ds(0, 15)], ss_q.at[3])
    c2.wait_send()


def hand_over(p_in, q_in, p_out, q_out):
    p_out[...] = p_in[...]
    q_out[...] = q_in[...]


def local(queries, keys, values, out_grad, q_init, lengths):
    dma = pltpu.SemaphoreType.DMA
    n = REACH + 1
    vm = pl.BlockSpec(memory_space=pltpu.VMEM)
    outs = pl.pallas_call(
        kernel,
        out_shape=(
            jax.ShapeDtypeStruct((RANK, WIDTH), F32),
            jax.ShapeDtypeStruct((RANK, D), F32),
        ),
        in_specs=[pl.BlockSpec(memory_space=pltpu.SMEM)] + [pl.BlockSpec(memory_space=pl.ANY)] * 5,
        out_specs=(vm, vm),
        scratch_shapes=[
            pltpu.VMEM((FR, WIDTH), BF16),
            pltpu.VMEM((FR, WIDTH), BF16),
            pltpu.VMEM((FR, WIDTH), BF16),
            pltpu.VMEM((FR, D), BF16),
            pltpu.VMEM((RANK, D), BF16),
            pltpu.VMEM((n, FR, WIDTH), BF16),
            pltpu.VMEM((n * HEADS, FR, FR), BF16),
            pltpu.VMEM((n * GROUPS * 8, FR), F32),
            pltpu.VMEM((GROUPS, n, 8, 128), F32),
            pltpu.VMEM((GROUPS, n, 8, 128), F32),
            pltpu.VMEM((GROUPS, 8, 128), F32),
            pltpu.VMEM((GROUPS, n, 8, 128), F32),
            pltpu.VMEM((n * GROUPS * 8, FR), F32),
            pltpu.VMEM((n, RANK, FR), BF16),
            pltpu.VMEM((n, RANK, FR), F32),
            pltpu.VMEM((n, RANK, FR), BF16),
            pltpu.VMEM((n, RANK, FR), BF16),
            pltpu.VMEM((GROUPS, 32, 8, 128), F32),
            pltpu.VMEM((GROUPS, 32, 8, 128), F32),
            pltpu.VMEM((GROUPS, 8, 8, 128), F32),
            pltpu.VMEM((GROUPS, 32, 8, 128), F32),
            pltpu.VMEM((RANK, D), F32),
            pltpu.VMEM((RANK, D // 2), F32),
            pltpu.VMEM((16, RANK, 128), BF16),
            pltpu.VMEM((16, RANK, 128), BF16),
            pltpu.VMEM((8, RANK, 128), BF16),
            pltpu.VMEM((2, 16, RANK, 128), BF16),
            dma((5,)), dma((7,)), dma((4,)), dma((4,)), dma((4,)), dma((4,)), dma((4,)), dma((5, 4)),
            dma((3, 7)), dma((2, 4)), dma((4, 4)),
            dma((5, GROUPS)), dma((5, GROUPS)), dma((3,)), dma((3,)), dma((5,)), dma((5,)),
        ],
        compiler_params=pltpu.CompilerParams(
            collective_id=0, has_side_effects=True, vmem_limit_bytes=60 << 20
        ),
        name="attend",
    )(lengths, queries[0], keys[0], values[0], out_grad[0], q_init)
    return pl.pallas_call(
        hand_over,
        out_shape=tuple(jax.ShapeDtypeStruct(o.shape, F32) for o in outs),
        in_specs=[vm] * 2,
        out_specs=(vm,) * 2,
        name="hand_over",
    )(*outs)


def solution(mesh):
    placed = (
        P("dp", "ctx", None),
        P("dp", "ctx", None),
        P("dp", "ctx", None),
        P("dp", "ctx", None),
        P(),
        P("dp"),
    )
    return jax.shard_map(local, mesh=mesh, in_specs=placed, out_specs=(P(), P()), check_vma=False)
```

```python
import functools

import jax
import jax.numpy as jnp
from jax import lax
from jax.experimental import pallas as pl
from jax.experimental.pallas import tpu as pltpu
from jax.sharding import PartitionSpec as P

HD = 128
FR = 256
HEADS = 16
WIDTH = HEADS * HD
D = 4096
RANK = 64
REACH = 8
GROUPS = 4
PER = HEADS // GROUPS
PARTS = GROUPS
CH = WIDTH // PARTS
LOG2E = 1.4426950408889634
SCALE2 = LOG2E / HD**0.5
LOW = -1e30
MESH = pl.DeviceIdType.MESH
F32 = jnp.float32
BF16 = jnp.bfloat16


def nt(a, b, **kw):
    return lax.dot_general(a, b, (((1,), (1,)), ((), ())), preferred_element_type=F32, **kw)


def nn(a, b, **kw):
    return lax.dot_general(a, b, (((1,), (0,)), ((), ())), preferred_element_type=F32, **kw)


def kernel(
    len_ref, q_any, k_any, v_any, g_any, qi_any, phat_ref, qnew_ref,
    q_ref, k_ref, v_ref, g_ref, qi_ref,
    qbuf, ebuf, mx, lg_out, lg_in, ls_out, ls_in, fac, pj_in, yacc, mp_out, mp_in,
    xp, xr, xz, psum, xq, xq_c, xq_b, xq_xy, xq_z, qg,
    ss_in, ss_x, ss_dm, ss_dp, ss_f1, ss_f3, ss_t, ss_sib, rs_slot, rs_h, rs_sib,
    ss_g, rs_g, ss_o, rs_o, ss_q, rs_q,
):
    dp = lax.axis_index("dp")
    ctx = lax.axis_index("ctx")
    zlo, y = dp // 4, dp % 4
    x, zh, core = ctx // 8, (ctx // 2) % 4, ctx % 2
    plane = x * 4 + y
    zz = zh * 2 + zlo
    rank = plane * 2 + core

    def at_ctx(i):
        return (dp, lax.rem(i + 64, 32))

    def at_plane(p):
        return (zlo * 4 + p % 4, (p // 4) * 8 + zh * 2 + core)

    def at_rank(r):
        return (zlo * 4 + (r // 2) % 4, (r // 8) * 8 + zh * 2 + r % 2)

    def at_z(z):
        return ((z % 2) * 4 + y, x * 8 + (z // 2) * 2 + core)

    sibling = (dp, ctx + 1 - 2 * core)
    up = (dp, x * 8 + ((zh + 1) % 4) * 2 + core)
    down = (dp, x * 8 + ((zh + 3) % 4) * 2 + core)
    left = at_ctx(ctx - 8)

    def rc(src, dst, ss, rs, device):
        return pltpu.make_async_remote_copy(
            src_ref=src, dst_ref=dst, send_sem=ss, recv_sem=rs, device_id=device, device_id_type=MESH
        )

    def each(lo, hi, do):
        def body(i, c):
            do(i)
            return c

        lax.fori_loop(lo, hi, body, 0)

    loads = [
        pltpu.make_async_copy(a, b, ss_in.at[i])
        for i, (a, b) in enumerate(
            ((q_any, q_ref), (k_any, k_ref), (g_any, g_ref), (qi_any, qi_ref), (v_any, v_ref))
        )
    ]
    for load in loads:
        load.start()

    bar = pltpu.get_barrier_semaphore()

    def greet(device):
        pl.semaphore_signal(bar, 1, device_id=device, device_id_type=MESH)

    def greet_ctx(i):
        greet(at_ctx(ctx + i))
        greet(at_ctx(ctx - i))

    each(1, REACH + 1, greet_ctx)
    each(1, 32, lambda i: greet(at_rank((rank + i) % 32)))
    each(1, 8, lambda i: greet(at_z((zz + i) % 8)))
    pl.semaphore_wait(bar, 2 * REACH + 31 + 7)

    def cols(g):
        return pl.ds(g * CH, CH)

    def chunk(d, g):
        return qbuf.at[d, :, cols(g)]

    mid = (zh == 1) | (zh == 2)
    edge = (zh == 0) | (zh == 3)

    def c_x(g):
        return rc(q_ref.at[:, cols(g)], chunk(8, g), ss_x.at[g], rs_slot.at[2, g], left)

    def sub(ref, p):
        return ref.at[:, pl.ds(p * CH // 4, CH // 4)]

    def c_x0(p):
        i = 0 if p == 0 else 3 + p
        return rc(sub(q_ref, p), sub(qbuf.at[8], p), ss_x.at[i], rs_slot.at[2, i], left)

    def pass_piece(p):
        src = sub(qbuf.at[8], p)

        @pl.when(zh == 0)
        def _():
            rc(src, sub(qbuf.at[2], p), ss_dm.at[0], rs_slot.at[0, 0], down).start()

        @pl.when(zh < 3)
        def _():
            rc(src, sub(qbuf.at[6], p), ss_dp.at[0], rs_slot.at[1, 0], up).start()

    def c_dm(g, own):
        src = q_ref.at[:, cols(g)] if own else chunk(8, g)
        return rc(src, chunk(2, g), ss_dm.at[g], rs_slot.at[0, g], down)

    def c_dp(g, own):
        src = q_ref.at[:, cols(g)] if own else chunk(8, g)
        return rc(src, chunk(6, g), ss_dp.at[g], rs_slot.at[1, g], up)

    def c_f1(g):
        slot, sem = jnp.where(zh == 0, 0, 4), jnp.where(zh == 0, 1, 0)
        return rc(chunk(2, g), chunk(slot, g), ss_f1.at[g], rs_h.at[sem, g], down)

    def c_f3(g):
        slot, sem = jnp.where(zh == 3, 0, 4), jnp.where(zh == 3, 1, 0)
        return rc(chunk(6, g), chunk(slot, g), ss_f3.at[g], rs_h.at[sem, g], up)

    def forwards(g):
        return edge if g < PARTS // 2 else mid

    def c_t(g):
        far = (dp, lax.rem(ctx + jnp.where(zh == 0, 8, 24), 32))
        return rc(chunk(0, g), chunk(4, g), ss_t.at[g], rs_h.at[0, g], far)

    def c_sib(k, g):
        if k == 0:
            src, to = q_ref.at[:, cols(g)], 1
        elif k == 4:
            src, to = chunk(8, g), 7
        else:
            src, to = chunk(2 * k, g), 2 * k - 1 + 2 * core
        return rc(src, chunk(to, g), ss_sib.at[k, g], rs_sib.at[(to - 1) // 2, g], sibling)

    def got(dst, rs):
        rc(dst, dst, ss_x.at[0], rs, sibling).wait_recv()

    def left_all(src, ss):
        rc(src, src, ss, rs_g.at[0, 0], sibling).wait_send()

    keep_row = lax.broadcasted_iota(jnp.int32, (FR, FR), 0)
    keep_col = lax.broadcasted_iota(jnp.int32, (FR, FR), 1)

    def fold(a):
        return jnp.concatenate([a[:, : FR // 2], a[:, FR // 2 :]], axis=0)

    def unfold(a):
        return jnp.concatenate([a[:PER], a[PER:]], axis=1)

    def stat(ref, d, g):
        return ref.at[pl.ds(pl.multiple_of((d * GROUPS + g) * 8, 8), 8), :]

    def unit(d, g):
        tops, sums = [], []
        for i in range(PER):
            h = g * PER + i
            hs = slice(h * HD, h * HD + HD)
            qh = q_ref[:, hs] if isinstance(d, int) and d == 0 else qbuf[d, :, hs]
            s = nt(k_ref[:, hs], qh)
            if isinstance(d, int) and d == 0:
                s = jnp.where(keep_row <= keep_col, s, LOW)
            elif isinstance(d, int) and d == 8:
                s = jnp.where(keep_row > keep_col, s, LOW)
            m = jnp.max(s, axis=0, keepdims=True)
            e = jnp.exp2((s - m) * SCALE2)
            ebuf[d * HEADS + h] = e.astype(BF16)
            tops.append(m)
            sums.append(jnp.sum(e, axis=0, keepdims=True))
        top = jnp.concatenate(tops, axis=0) * SCALE2
        logs = top + jnp.log2(jnp.concatenate(sums, axis=0))
        stat(mx, d, g)[...] = jnp.concatenate([top, top], axis=0)
        lg_out[g, d] = fold(logs)

    def early_odd(g):
        for k in (0, 3, 1 + core):
            on_sib(g, k)
        unit(1, g)
        unit(7, g)
        unit(3 + 2 * core, g)

    def on_x(g):
        if g == 0:
            for p in range(4):
                got(sub(qbuf.at[8], p), rs_slot.at[2, 0 if p == 0 else 3 + p])
                pass_piece(p)
        else:
            got(chunk(8, g), rs_slot.at[2, g])

        @pl.when(core == 0)
        def _():
            c_sib(4, g).start()

    def on_1(g):
        got(chunk(2, g), rs_slot.at[0, g])
        pl.when(forwards(g))(lambda: c_f1(g).start())
        c_sib(1, g).start()

    def on_3(g):
        got(chunk(6, g), rs_slot.at[1, g])
        pl.when(forwards(g))(lambda: c_f3(g).start())
        c_sib(3, g).start()

    def on_t(g):
        @pl.when(edge)
        def _():
            got(chunk(0, g), rs_h.at[1, g])
            c_t(g).start()

    def on_2(g):
        got(chunk(4, g), rs_h.at[0, g])
        c_sib(2, g).start()

    def on_sib(g, k):
        got(chunk(2 * k + 1, g), rs_sib.at[k, g])

    def c_lg(d, g):
        return rc(lg_out.at[g, d], lg_in.at[g, d], ss_g.at[0, g], rs_g.at[0, g], at_ctx(ctx + d))

    def c_ls(d, g):
        return rc(ls_out.at[g], ls_in.at[g, d], ss_g.at[1, g], rs_g.at[1, g], at_ctx(ctx - d))

    def c_p(k):
        return rc(pj_in.at[0], pj_in.at[2 * k], ss_o.at[0], rs_o.at[0], at_ctx(ctx - 2 * k))

    def c_ps(k):
        src, to = (pj_in.at[0], 1) if k == 0 else (pj_in.at[2 * k], 2 * k - 1 + 2 * core)
        if k == 4:
            to = 7
        return rc(src, pj_in.at[to], ss_o.at[2], rs_o.at[2], sibling)

    def share_proj():
        got(pj_in.at[pl.ds(1, 4)], rs_o.at[0])
        for k in (1, 2, 3):
            c_ps(k).start()

        @pl.when(core == 0)
        def _():
            c_ps(4).start()

        @pl.when(core == 1)
        def _():
            c_ps(0).start()

    def c_m(d):
        return rc(mp_out.at[d], mp_in.at[d], ss_o.at[1], rs_o.at[1], at_ctx(ctx + d))

    def stage_a(g):
        each(1, REACH + 1, lambda d: c_lg(d, g).start())

    def stage_b(g):
        got(lg_in.at[g, pl.ds(1, REACH)], rs_g.at[0, g])
        logs = [lg_out[g, 0]]
        for d in range(1, REACH + 1):
            logs.append(jnp.where(ctx >= d, lg_in[g, d], LOW))
        top = functools.reduce(jnp.maximum, logs)
        total = functools.reduce(jnp.add, [jnp.exp2(a - top) for a in logs])
        ls_out[g] = top + jnp.log2(total)
        each(1, REACH + 1, lambda d: c_ls(d, g).start())

    def c_rs(k, g):
        r = (rank + k) % 32
        return rc(xp.at[g, r], xr.at[g, rank], ss_g.at[2, g], rs_g.at[2, g], at_rank(r))

    def c_z(k, g):
        return rc(xz.at[g, zz], xz.at[g, zz], ss_g.at[3, g], rs_g.at[3, g], at_z((zz + k) % 8))

    def c_ag(k, g):
        ref = psum.at[g, rank]
        return rc(ref, ref, ss_g.at[4, g], rs_g.at[4, g], at_rank((rank + k) % 32))

    def stage_c(g):
        got(ls_in.at[g, pl.ds(1, REACH)], rs_g.at[1, g])
        lane = lax.broadcasted_iota(jnp.int32, (PER, FR), 1)
        accs = [jnp.zeros((RANK, FR), F32) for _ in range(PER)]
        for d in range(REACH + 1):
            ls = unfold(ls_out[g] if d == 0 else ls_in[g, d])
            pos = (ctx + d) * FR + lane
            f = jnp.exp2(stat(mx, d, g)[...][:PER] - ls)
            f = jnp.where((pos < len_ref[0]) & (ctx + d < 32), f, 0.0)
            stat(fac, d, g)[...] = jnp.concatenate([f, f], axis=0)
            pj = pj_in[d].astype(F32)
            for i in range(PER):
                pf = (pj * f[i : i + 1, :]).astype(BF16)
                accs[i] = accs[i] + nt(pf, ebuf[d * HEADS + g * PER + i])
        for i in range(PER):
            hs = slice((g * PER + i) * HD, (g * PER + i + 1) * HD)
            xp[g, 8 * i : 8 * i + 8] = nn(accs[i].astype(BF16), v_ref[:, hs]).reshape(8, 8, HD)
        each(1, 32, lambda k: c_rs(k, g).start())

    def stage_f(g):
        xr[g, rank] = xp[g, rank]
        got(xr.at[g, pl.ds(0, 31)], rs_g.at[2, g])
        total = xr[g, 0]
        for r in range(1, 32):
            total = total + xr[g, r]
        xz[g, zz] = total
        each(1, 8, lambda k: c_z(k, g).start())

    def stage_g(g):
        got(xz.at[g, pl.ds(0, 7)], rs_g.at[3, g])
        total = xz[g, 0]
        for z in range(1, 8):
            total = total + xz[g, z]
        psum[g, rank] = total
        each(1, 32, lambda k: c_ag(k, g).start())

    def p_head(g, i):
        return psum[g, 8 * i : 8 * i + 8].reshape(RANK, HD)

    def stage_i(g):
        got(psum.at[g, pl.ds(0, 31)], rs_g.at[4, g])
        us = []
        for i in range(PER):
            hs = slice((g * PER + i) * HD, (g * PER + i + 1) * HD)
            us.append(nt(p_head(g, i).astype(BF16), v_ref[:, hs]).astype(BF16))

        def part_of(d, start):
            f = stat(fac, d, g)[...]
            acc = start
            for i in range(PER):
                acc = acc + nn(us[i], ebuf[d * HEADS + g * PER + i]) * f[i : i + 1, :]
            return acc

        for i in range(REACH + 1):
            d = REACH - i
            acc = part_of(d, jnp.zeros((RANK, FR), F32) if g == 0 else yacc[d])
            if g < GROUPS - 1 or d == 0:
                yacc[d] = acc
            else:
                mp_out[d] = acc.astype(BF16)
                c_m(d).start()

    loads[0].wait()
    for g in range(PARTS):
        if g == 0:
            for p in range(4):
                c_x0(p).start()
        else:
            c_x(g).start()

        @pl.when(core == 1)
        def _():
            c_sib(0, g).start()

    early = PARTS // 2

    def own_down(g):
        pl.when(zh > 0)(lambda: c_dm(g, True).start())

    def own_up(g):
        pl.when(zh == 3)(lambda: c_dp(g, True).start())

    for g in range(PARTS):
        own_down(g)
        if g < early:
            own_up(g)

    def pass_on(g):
        if g < early:
            pl.when(zh == 0)(lambda: c_dm(g, False).start())
        pl.when(zh < 3)(lambda: c_dp(g, False).start())

    def late_down():
        for g in range(early, PARTS):
            pl.when(zh == 0)(lambda: c_dm(g, False).start())

    def late_up():
        for g in range(early, PARTS):
            own_up(g)

    for load in loads[1:4]:
        load.wait()
    pj_in[0] = nt(qi_ref[...], g_ref[...]).astype(BF16)
    each(1, 5, lambda k: c_p(k).start())
    loads[4].wait()
    on_x(0)
    on_x(1)
    pass_on(1)
    unit(0, 0)
    unit(8, 0)
    on_1(0)
    on_x(2)
    pass_on(2)
    on_3(0)
    unit(0, 1)
    unit(8, 1)
    on_x(3)
    pass_on(3)
    on_1(1)
    late_down()
    on_3(1)
    late_up()
    unit(0, 2)
    unit(8, 2)
    unit(0, 3)
    unit(8, 3)
    unit(2, 0)
    unit(6, 0)
    early_odd(0)
    on_t(0)
    unit(2, 1)
    unit(6, 1)
    early_odd(1)
    on_1(2)
    on_3(2)
    on_t(1)
    unit(2, 2)
    unit(6, 2)
    early_odd(2)
    on_1(3)
    on_3(3)
    unit(2, 3)
    unit(6, 3)
    early_odd(3)

    def complete(g):
        on_2(g)
        unit(4, g)
        on_sib(g, 2 - core)
        unit(5 - 2 * core, g)
        stage_a(g)

    complete(0)
    share_proj()
    complete(2)
    complete(1)
    got(pj_in.at[pl.ds(1, 4)], rs_o.at[2])
    stage_b(0)
    complete(3)
    stage_b(2)
    stage_b(1)
    stage_c(0)
    stage_b(3)
    stage_c(2)
    stage_c(1)
    stage_c(3)
    stage_f(0)
    stage_f(2)
    stage_f(1)
    stage_f(3)
    stage_g(0)
    stage_g(2)
    stage_g(1)
    stage_g(3)
    stage_i(0)
    stage_i(1)
    stage_i(2)
    stage_i(3)

    p_sum = jnp.concatenate([p_head(g, i) for g in range(GROUPS) for i in range(PER)], axis=1)
    gram = nt(p_sum, p_sum, precision=lax.Precision.HIGHEST)
    row_i = lax.broadcasted_iota(jnp.int32, (RANK, 2 * RANK), 0)
    col_i = lax.broadcasted_iota(jnp.int32, (RANK, 2 * RANK), 1)
    a = jnp.concatenate([gram, jnp.zeros((RANK, RANK), F32)], axis=1)
    a = jnp.where(col_i == row_i + RANK, 1.0, a)
    pivots = jnp.zeros((RANK, 2 * RANK), F32)
    for k in range(RANK):
        wide = jnp.broadcast_to(a[:, k : k + 1], (RANK, 2 * RANK))
        piv = wide[k : k + 1, :]
        line = a[k : k + 1, :] / piv
        pivots = jnp.where(row_i == k, piv, pivots)
        a = a - jnp.where(row_i > k, wide, 0.0) * line
    inv_low = a[:, RANK:] * (lax.rsqrt(pivots[:, RANK:]) * (WIDTH**0.5))

    got(mp_in.at[pl.ds(1, REACH)], rs_o.at[1])
    acc = yacc[0]
    for d in range(1, REACH + 1):
        acc = acc + jnp.where(ctx >= d, mp_in[d].astype(F32), 0.0)
    mapped = nn(inv_low, acc, precision=lax.Precision.HIGHEST).astype(BF16)

    half_w = D // 2
    mine = pl.ds(pl.multiple_of(core * half_w, half_w), half_w)
    step = 512

    def q_cols(base, i):
        s = pl.ds(pl.multiple_of(base + i * step, step), step)
        xq[:, s] = nn(mapped, g_ref[:, s])

    quarter = half_w // 2

    def c_cc(p):
        src = pl.ds(pl.multiple_of((1 - core) * half_w + p * quarter, quarter), quarter)
        dst = xq_c.at[:, pl.ds(p * quarter, quarter)]
        return rc(xq.at[:, src], dst, ss_q.at[5 * p], rs_q.at[5 * p], sibling)

    for p in range(2):
        each(2 * p, 2 * p + 2, lambda i: q_cols((1 - core) * half_w, i))
        c_cc(p).start()
    each(0, half_w // step, lambda i: q_cols(core * half_w, i))
    for p in range(2):
        c_cc(p).wait_recv()

    def join(i):
        s = pl.ds(pl.multiple_of(i * 128, 128), 128)
        t = pl.ds(pl.multiple_of(core * half_w + i * 128, 128), 128)
        xq_b[i] = (xq_c[:, s] + xq[:, t]).astype(BF16)

    def c_qx(k):
        p = (plane + k) % 16
        return rc(xq_b.at[p], xq_xy.at[plane], ss_q.at[1], rs_q.at[1], at_plane(p))

    def join_send(k):
        join((plane + k) % 16)
        c_qx(k).start()

    each(1, 16, join_send)
    join(plane)
    xq_xy[plane] = xq_b[plane]
    got(xq_xy.at[pl.ds(0, 15)], rs_q.at[1])
    total = xq_xy[0].astype(F32)
    for p in range(1, 16):
        total = total + xq_xy[p].astype(F32)
    xq_z[zz] = total.astype(BF16)

    def c_qz(k):
        return rc(xq_z.at[zz], xq_z.at[zz], ss_q.at[2], rs_q.at[2], at_z((zz + k) % 8))

    each(1, 8, lambda k: c_qz(k).start())
    phat_ref[...] = nn(inv_low, p_sum, precision=lax.Precision.HIGHEST)
    got(xq_z.at[pl.ds(0, 7)], rs_q.at[2])
    total = xq_z[0].astype(F32)
    for z in range(1, 8):
        total = total + xq_z[z].astype(F32)
    done = total * (1.0 / 256.0)
    qg[core, plane] = done.astype(BF16)

    def c_qa(k):
        ref = qg.at[core, plane]
        return rc(ref, ref, ss_q.at[3], rs_q.at[3], at_plane((plane + k) % 16))

    each(1, 16, lambda k: c_qa(k).start())
    got(qg.at[core, pl.ds(0, 15)], rs_q.at[3])
    c2 = rc(qg.at[core], qg.at[core], ss_q.at[4], rs_q.at[4], sibling)
    c2.start()
    for j in (core, 1 - core):
        if j is not core:
            got(qg.at[j], rs_q.at[4])
        for i in range(16):
            s = pl.ds(pl.multiple_of(j * half_w + i * 128, 128), 128)
            qnew_ref[:, s] = qg[j, i].astype(F32)

    for g in range(PARTS):
        if g == 0:
            for p in range(4):
                c_x0(p).wait_send()
        else:
            c_x(g).wait_send()
        c_dm(g, True).wait_send()
        c_dp(g, True).wait_send()

        @pl.when(forwards(g))
        def _():
            c_f1(g).wait_send()
            c_f3(g).wait_send()

        for k in (1, 2, 3):
            c_sib(k, g).wait_send()

        if g < PARTS // 2:

            @pl.when(edge)
            def _():
                c_t(g).wait_send()

        @pl.when(core == 1)
        def _():
            c_sib(0, g).wait_send()

        @pl.when(core == 0)
        def _():
            c_sib(4, g).wait_send()

    for g in range(GROUPS):
        left_all(lg_in.at[g, pl.ds(0, REACH)], ss_g.at[0, g])
        left_all(ls_in.at[g, pl.ds(0, REACH)], ss_g.at[1, g])
        left_all(xr.at[g, pl.ds(0, 31)], ss_g.at[2, g])
        left_all(xz.at[g, pl.ds(0, 7)], ss_g.at[3, g])
        left_all(psum.at[g, pl.ds(0, 31)], ss_g.at[4, g])
    left_all(pj_in.at[pl.ds(0, 4)], ss_o.at[0])
    left_all(pj_in.at[pl.ds(0, 4)], ss_o.at[2])
    left_all(mp_in.at[pl.ds(0, REACH)], ss_o.at[1])
    for p in range(2):
        c_cc(p).wait_send()
    left_all(xq_xy.at[pl.ds(0, 15)], ss_q.at[1])
    left_all(xq_z.at[pl.ds(0, 7)], ss_q.at[2])
    left_all(qg.at[core, pl.ds(0, 15)], ss_q.at[3])
    c2.wait_send()


def hand_over(p_in, q_in, p_out, q_out):
    p_out[...] = p_in[...]
    q_out[...] = q_in[...]


def local(queries, keys, values, out_grad, q_init, lengths):
    dma = pltpu.SemaphoreType.DMA
    n = REACH + 1
    vm = pl.BlockSpec(memory_space=pltpu.VMEM)
    outs = pl.pallas_call(
        kernel,
        out_shape=(
            jax.ShapeDtypeStruct((RANK, WIDTH), F32),
            jax.ShapeDtypeStruct((RANK, D), F32),
        ),
        in_specs=[pl.BlockSpec(memory_space=pltpu.SMEM)] + [pl.BlockSpec(memory_space=pl.ANY)] * 5,
        out_specs=(vm, vm),
        scratch_shapes=[
            pltpu.VMEM((FR, WIDTH), BF16),
            pltpu.VMEM((FR, WIDTH), BF16),
            pltpu.VMEM((FR, WIDTH), BF16),
            pltpu.VMEM((FR, D), BF16),
            pltpu.VMEM((RANK, D), BF16),
            pltpu.VMEM((n, FR, WIDTH), BF16),
            pltpu.VMEM((n * HEADS, FR, FR), BF16),
            pltpu.VMEM((n * GROUPS * 8, FR), F32),
            pltpu.VMEM((GROUPS, n, 8, 128), F32),
            pltpu.VMEM((GROUPS, n, 8, 128), F32),
            pltpu.VMEM((GROUPS, 8, 128), F32),
            pltpu.VMEM((GROUPS, n, 8, 128), F32),
            pltpu.VMEM((n * GROUPS * 8, FR), F32),
            pltpu.VMEM((n, RANK, FR), BF16),
            pltpu.VMEM((n, RANK, FR), F32),
            pltpu.VMEM((n, RANK, FR), BF16),
            pltpu.VMEM((n, RANK, FR), BF16),
            pltpu.VMEM((GROUPS, 32, 8, 128), F32),
            pltpu.VMEM((GROUPS, 32, 8, 128), F32),
            pltpu.VMEM((GROUPS, 8, 8, 128), F32),
            pltpu.VMEM((GROUPS, 32, 8, 128), F32),
            pltpu.VMEM((RANK, D), F32),
            pltpu.VMEM((RANK, D // 2), F32),
            pltpu.VMEM((16, RANK, 128), BF16),
            pltpu.VMEM((16, RANK, 128), BF16),
            pltpu.VMEM((8, RANK, 128), BF16),
            pltpu.VMEM((2, 16, RANK, 128), BF16),
            dma((5,)), dma((7,)), dma((4,)), dma((4,)), dma((4,)), dma((4,)), dma((4,)), dma((5, 4)),
            dma((3, 7)), dma((2, 4)), dma((4, 4)),
            dma((5, GROUPS)), dma((5, GROUPS)), dma((3,)), dma((3,)), dma((6,)), dma((6,)),
        ],
        compiler_params=pltpu.CompilerParams(
            collective_id=0, has_side_effects=True, vmem_limit_bytes=60 << 20
        ),
        name="attend",
    )(lengths, queries[0], keys[0], values[0], out_grad[0], q_init)
    return pl.pallas_call(
        hand_over,
        out_shape=tuple(jax.ShapeDtypeStruct(o.shape, F32) for o in outs),
        in_specs=[vm] * 2,
        out_specs=(vm,) * 2,
        name="hand_over",
    )(*outs)


def solution(mesh):
    placed = (
        P("dp", "ctx", None),
        P("dp", "ctx", None),
        P("dp", "ctx", None),
        P("dp", "ctx", None),
        P(),
        P("dp"),
    )
    return jax.shard_map(local, mesh=mesh, in_specs=placed, out_specs=(P(), P()), check_vma=False)
```
